256 devices in a mesh: dp: 4 (over y_lo, core), seq: 64 (over x, z, y_hi).
Axes of the slice: x: 4, y: 4 (y_hi: 2, y_lo: 2; y = y_hi * 2 + y_lo), z: 8, core: 2. Of those that a mesh axis runs over, the one named last changes fastest.
Arguments:
- latents: bfloat16 [4, 64, 256, 1152], P('dp', 'seq'), may hold values from -6 to 6
- out_grad: bfloat16 [4, 64, 256, 1152], P('dp', 'seq'), may hold values from -16 to 16
- qkv_spatial: bfloat16 [1728, 1152], replicated, may hold values from -4 to 4
- proj_spatial: bfloat16 [1152, 576], replicated, may hold values from -0.25 to 0.25
- qkv_temporal: bfloat16 [1728, 1152], replicated, may hold values from -4 to 4
- proj_temporal: bfloat16 [1152, 576], replicated, may hold values from -0.25 to 0.25
Outputs:
- latents_grad: bfloat16 [4, 64, 256, 1152], P('dp', 'seq')
- qkv_spatial_grad: float32 [1728, 1152], P('seq', 'dp')
- proj_spatial_grad: float32 [1152, 576], P('seq', 'dp')
- qkv_temporal_grad: float32 [1728, 1152], P('seq', 'dp')
- proj_temporal_grad: float32 [1152, 576], P('seq', 'dp')
The draws below stay inside these ranges and needn't reach their ends.
All inputs are finite; a program needn't handle non-finite values.
Results may differ from the reference program's by a relative error of at most 0.025.
Values may be sent and summed in bfloat16 or wider, within the bound.
A program may use at most 128 MiB of HBM per device.

```python
import jax
import jax.numpy as jnp
from jax import lax

D = 1152
HDIM = 72
SPATIAL = 256
HD = 576
FRAMES = 64
VIDEOS = 4


def draw_qkv_spatial(key, part):
    key = jax.random.fold_in(key, 11)
    return (jax.random.normal(key, (3 * HD, D), jnp.float32) * D ** (-0.5)).astype(jnp.bfloat16)


def draw_qkv_temporal(key, part):
    key = jax.random.fold_in(key, 23)
    return (jax.random.normal(key, (3 * HD, D), jnp.float32) * D ** (-0.5)).astype(jnp.bfloat16)


def with_spikes(values, own_key, source, target, blocks, factor):
    def block_of(axis_at):
        return (jnp.arange(values.shape[axis_at]) // (values.shape[axis_at] // blocks)).reshape((-1,) + (1,) * (values.ndim - 1 - axis_at))

    first = jax.random.permutation(own_key, blocks)[block_of(target)]
    far = (block_of(target) + blocks // 2) % blocks
    return jnp.where((block_of(source) == first) | (block_of(source) == far), factor * values, values)


def steps_of(stream_key, shape, shards, least, high):
    def one(dim, blocks):
        draws = jax.random.uniform(jax.random.fold_in(jax.random.fold_in(stream_key, 6), dim), (blocks,), jnp.float32, least / len(shards), high / len(shards))
        return jnp.repeat(jnp.exp(draws), shape[dim] // blocks).reshape((-1,) + (1,) * (len(shape) - dim - 1))

    loudness = one(*shards[0])
    for cut in shards[1:]:
        loudness = loudness * one(*cut)
    return loudness


def scatter_about(own_key, extent, scale, reach, cuts=(), kind=jnp.bfloat16):
    values = scale * jax.random.normal(own_key, extent, jnp.float32)
    if cuts:
        values = values * steps_of(own_key, extent, cuts, -0.22, 0.18)
    return jnp.clip(values, -reach, reach).astype(kind)


def bell_draw_with(key, shape, scale, most, split, heavy, held_as=jnp.bfloat16):
    values = scale * jax.random.normal(key, shape, jnp.float32)
    if split:
        values = values * steps_of(key, shape, split, -0.22, 0.18)
    return jnp.clip(with_spikes(values, jax.random.fold_in(key, 3), *heavy), -most, most).astype(held_as)


def setup_inputs(seed: int = 0) -> dict:
    streams_of = jax.random.split(jax.random.key(seed), 7)
    return {
        "latents": scatter_about(streams_of[0], (VIDEOS, FRAMES, SPATIAL, D), 1.0, 6.0, ((0, 4), (1, 64))),
        "out_grad": bell_draw_with(streams_of[1], (VIDEOS, FRAMES, SPATIAL, D), 1.0, 16.0, ((0, 4), (1, 64)), (1, 3, 64, 4.0)),
        "qkv_spatial": draw_qkv_spatial(jax.random.fold_in(streams_of[6], 71), 0),
        "proj_spatial": scatter_about(streams_of[3], (D, HD), HD ** -0.5, 0.25),
        "qkv_temporal": draw_qkv_temporal(jax.random.fold_in(streams_of[6], 71), 0),
        "proj_temporal": scatter_about(streams_of[5], (D, HD), HD ** -0.5, 0.25),
    }


EPS = 1e-06

def normalize(source):
    widened = source.astype(jnp.float32)
    inverse = lax.rsqrt(lax.optimization_barrier(jnp.mean(widened * widened, axis=-1, keepdims=True)) + EPS)
    return (widened, widened * inverse, inverse)

def split_heads(packed):
    return packed.astype(jnp.float32).reshape(packed.shape[:-1] + (packed.shape[-1] // HDIM, HDIM))

def attend(query, keys, values, layout):
    key_layout = layout.replace('l', 'm')
    scale = HDIM ** (-0.5)
    scores = jnp.einsum(layout + ',' + key_layout + '->bhlm', split_heads(query), split_heads(keys)) * scale
    attn_probs = jax.nn.softmax(scores, axis=-1)
    rounded = attn_probs.astype(jnp.bfloat16)
    attn_out = jnp.einsum('bhlm,' + key_layout + '->' + layout, rounded.astype(jnp.float32), split_heads(values))
    return (attn_out.astype(jnp.bfloat16).reshape(query.shape), attn_probs, rounded)

def block_forward(source, qkv_weight, out_weight, layout):
    widened, normed, inverse = normalize(source)
    hidden = normed.astype(jnp.bfloat16)
    width_d = source.shape[-1]
    flat = hidden.reshape(-1, width_d)
    packed = jnp.dot(flat, qkv_weight.T, preferred_element_type=jnp.float32).astype(jnp.bfloat16)
    packed = packed.reshape(source.shape[:-1] + (qkv_weight.shape[0],))
    width = packed.shape[-1] // 3
    query = packed[..., :width]
    keys = packed[..., width:2 * width]
    values = packed[..., 2 * width:]
    attn_out, attn_probs, rounded = attend(query, keys, values, layout)
    branch = jnp.dot(attn_out.reshape(-1, width), out_weight.T, preferred_element_type=jnp.float32)
    result = (widened + branch.reshape(source.shape)).astype(jnp.bfloat16)
    return (result, (hidden, normed, inverse, query, keys, values, attn_out, attn_probs, rounded))

def attend_back(d_attn, query, keys, values, attn_out, attn_probs, rounded, layout):
    key_layout = layout.replace('l', 'm')
    scale = HDIM ** (-0.5)
    grad_heads = split_heads(d_attn)
    d_probs = jnp.einsum(layout + ',' + key_layout + '->bhlm', grad_heads, split_heads(values))
    d_values = jnp.einsum('bhlm,' + layout + '->' + key_layout, rounded.astype(jnp.float32), grad_heads)
    offset = jnp.einsum(layout + ',' + layout + '->bhl', grad_heads, split_heads(attn_out))
    d_scores = (attn_probs * (d_probs - offset[..., None]) * scale).astype(jnp.bfloat16).astype(jnp.float32)
    d_query = jnp.einsum('bhlm,' + key_layout + '->' + layout, d_scores, split_heads(keys))
    d_keys = jnp.einsum('bhlm,' + layout + '->' + key_layout, d_scores, split_heads(query))
    pieces = [d_query.reshape(query.shape), d_keys.reshape(query.shape), d_values.reshape(query.shape)]
    return jnp.concatenate(pieces, axis=-1).astype(jnp.bfloat16)

def block_backward(d_next, qkv_weight, out_weight, saved, layout):
    hidden, normed, inverse, query, keys, values, attn_out, attn_probs, rounded = saved
    width_d = d_next.shape[-1]
    flat_grad = d_next.reshape(-1, width_d)
    flat_attn = attn_out.reshape(-1, attn_out.shape[-1])
    out_grad_w = jnp.dot(flat_grad.T, flat_attn, preferred_element_type=jnp.float32)
    d_attn = jnp.dot(flat_grad, out_weight, preferred_element_type=jnp.float32).astype(jnp.bfloat16)
    d_attn = d_attn.reshape(attn_out.shape)
    d_packed = attend_back(d_attn, query, keys, values, attn_out, attn_probs, rounded, layout)
    flat_packed = d_packed.reshape(-1, d_packed.shape[-1])
    qkv_grad_w = jnp.dot(flat_packed.T, hidden.reshape(-1, width_d), preferred_element_type=jnp.float32)
    d_hidden = jnp.dot(flat_packed, qkv_weight, preferred_element_type=jnp.float32).reshape(d_next.shape)
    d_source = d_next.astype(jnp.float32) + inverse * (d_hidden - normed * lax.optimization_barrier(jnp.mean(d_hidden * normed, axis=-1, keepdims=True)))
    return (d_source.astype(jnp.bfloat16), qkv_grad_w, out_grad_w)

def reference(latents, out_grad, qkv_spatial, proj_spatial, qkv_temporal, proj_temporal):

    def one_video(totals, pair):
        source, upstream = pair
        residual, saved_space = block_forward(source, qkv_spatial, proj_spatial, 'blhd')
        unused, saved_time = block_forward(residual, qkv_temporal, proj_temporal, 'lbhd')
        d_residual, qkv_time, out_time = block_backward(upstream, qkv_temporal, proj_temporal, saved_time, 'lbhd')
        d_source, qkv_space, out_space = block_backward(d_residual, qkv_spatial, proj_spatial, saved_space, 'blhd')
        summed = (totals[0] + qkv_space, totals[1] + out_space, totals[2] + qkv_time, totals[3] + out_time)
        return (summed, d_source)
    start = (jnp.zeros(qkv_spatial.shape, jnp.float32), jnp.zeros(proj_spatial.shape, jnp.float32), jnp.zeros(qkv_temporal.shape, jnp.float32), jnp.zeros(proj_temporal.shape, jnp.float32))
    totals, latents_grad = lax.scan(one_video, start, (latents, out_grad))
    return (latents_grad, totals[0], totals[1], totals[2], totals[3])
```

```python
import functools

import jax
import jax.numpy as jnp
from jax import lax
from jax.experimental import pallas as pl
from jax.experimental.pallas import tpu as pltpu
from jax.sharding import PartitionSpec as P

HDIM = 72
HEADS = 8
HD = HDIM * HEADS
PAD = 640
D = 1152
TOK = 256
GROUPS = 64
OWN = TOK // GROUPS
EPS = 1e-06
SCALE = HDIM ** (-0.5)
NEG = -1e30
MESH = pl.DeviceIdType.MESH
VMEM = pltpu.VMEM
F32 = jnp.float32
BF16 = jnp.bfloat16
LIMIT = 56 * 2**20

QROWS = 288
PROWS = 96
ROWS = QROWS + PROWS
LANES = 2048


def dot(a, b, dims=((1,), (0,))):
    return lax.dot_general(a, b, (dims, ((), ())), preferred_element_type=F32)


NT = ((1,), (1,))
TN = ((0,), (0,))


def window(head):
    low = head * HDIM // 128 * 128
    return low, -(-(head + 1) * HDIM // 128) * 128


def head_mask(head, low, high):
    lane = lax.broadcasted_iota(jnp.int32, (1, high - low), 1) + low
    return ((lane >= head * HDIM) & (lane < (head + 1) * HDIM)).astype(F32).astype(BF16)


def normalize(x):
    inverse = lax.rsqrt(jnp.mean(x * x, axis=-1, keepdims=True) + EPS)
    return x * inverse, inverse


def project(hidden, w_ref, targets):
    for i, target in enumerate(targets):
        target[:, :HD] = dot(hidden, w_ref[i * HD : (i + 1) * HD, :], NT).astype(BF16)
        target[:, HD:] = jnp.zeros((TOK, PAD - HD), BF16)


def softmax(qm, k, keep):
    s = dot(qm, k, NT) * SCALE
    if keep is not None:
        s = jnp.where(keep, s, NEG)
    e = jnp.exp(s - jnp.max(s, axis=-1, keepdims=True))
    return e * (1.0 / jnp.sum(e, axis=-1, keepdims=True))


def same_position():
    rows = lax.broadcasted_iota(jnp.int32, (TOK, TOK), 0)
    columns = lax.broadcasted_iota(jnp.int32, (TOK, TOK), 1)
    return lax.rem(rows, OWN) == lax.rem(columns, OWN)


def attention(q, k, v, acc, attn, keep):
    acc[...] = jnp.zeros_like(acc)
    for h in range(HEADS):
        low, high = window(h)
        mask = head_mask(h, low, high)
        probs = softmax(q[:, low:high] * mask, k[:, low:high], keep)
        acc[:, low:high] += dot(probs.astype(BF16), v[:, low:high] * mask)
    attn[...] = acc[...].astype(BF16)


def attention_back(q, k, v, attn, da, accs, keep):
    for acc in accs:
        acc[...] = jnp.zeros_like(acc)
    dq, dk, dv = accs
    for h in range(HEADS):
        low, high = window(h)
        mask = head_mask(h, low, high)
        qm = q[:, low:high] * mask
        km = k[:, low:high] * mask
        dam = da[:, low:high] * mask
        probs = softmax(qm, k[:, low:high], keep)
        d_probs = dot(dam, v[:, low:high], NT)
        dv[:, low:high] += dot(probs.astype(BF16), dam, TN)
        offset = jnp.sum(dam.astype(F32) * attn[:, low:high].astype(F32), axis=-1, keepdims=True)
        ds = (probs * (d_probs - offset) * SCALE).astype(BF16)
        dq[:, low:high] += dot(ds, km)
        dk[:, low:high] += dot(ds, qm, TN)


def block_back(dy, normed, inverse, w_ref, accs, dpk):
    d_hidden = jnp.zeros((TOK, D), F32)
    for i, acc in enumerate(accs):
        rounded = acc[...].astype(BF16)
        dpk[:, i * PAD : (i + 1) * PAD] = rounded
        d_hidden = d_hidden + dot(rounded[:, :HD], w_ref[i * HD : (i + 1) * HD, :])
    along = jnp.mean(d_hidden * normed, axis=-1, keepdims=True)
    return dy.astype(F32) + inverse * (d_hidden - normed * along)


def to_blocks(value, ref):
    for t in range(D // 128):
        ref[:, t, :, :] = value[:, t * 128 : (t + 1) * 128].reshape(GROUPS, OWN, 128)


def from_blocks(ref):
    return jnp.concatenate([ref[:, t, :, :].reshape(TOK, 128) for t in range(D // 128)], axis=1)


def space_forward(x_ref, dy_ref, w_ref, p_ref, next_ref, dyb_ref, q, k, v, attn, acc):
    to_blocks(dy_ref[...], dyb_ref)
    x = x_ref[...].astype(F32)
    normed, _ = normalize(x)
    project(normed.astype(BF16), w_ref, (q, k, v))
    attention(q, k, v, acc, attn, None)
    out = (x + dot(attn[:, :HD], p_ref[...], NT)).astype(BF16)
    to_blocks(out, next_ref)


def time_both(xb_ref, dyb_ref, w_ref, p_ref, dxb_ref, dy_out, ht, at, dpk, q, k, v, attn, da, a0, a1, a2):
    x = from_blocks(xb_ref).astype(F32)
    dy = from_blocks(dyb_ref)
    dy_out[...] = dy
    normed, inverse = normalize(x)
    hidden = normed.astype(BF16)
    ht[...] = hidden.T
    project(hidden, w_ref, (q, k, v))
    keep = same_position()
    attention(q, k, v, a0, attn, keep)
    at[...] = attn[...].T
    da[:, :HD] = dot(dy, p_ref[...]).astype(BF16)
    da[:, HD:] = jnp.zeros((TOK, PAD - HD), BF16)
    attention_back(q, k, v, attn, da, (a0, a1, a2), keep)
    to_blocks(block_back(dy, normed, inverse, w_ref, (a0, a1, a2), dpk).astype(BF16), dxb_ref)


def space_back(x_ref, dyb_ref, w_ref, p_ref, q, k, v, attn, dx_ref, dy_out, ht, at, dpk, da, a0, a1, a2):
    x = x_ref[...].astype(F32)
    dy = from_blocks(dyb_ref)
    dy_out[...] = dy
    normed, inverse = normalize(x)
    ht[...] = normed.astype(BF16).T
    at[...] = attn[...].T
    da[:, :HD] = dot(dy, p_ref[...]).astype(BF16)
    da[:, HD:] = jnp.zeros((TOK, PAD - HD), BF16)
    attention_back(q, k, v, attn, da, (a0, a1, a2), None)
    dx_ref[...] = block_back(dy, normed, inverse, w_ref, (a0, a1, a2), dpk).astype(BF16)


def shape(*dims, dtype=BF16):
    return jax.ShapeDtypeStruct(dims, dtype)


ANYV = pl.BlockSpec(memory_space=VMEM)


def call(body, ins, outs, scratch, name, collective=None):
    return pl.pallas_call(
        body,
        out_shape=outs,
        in_specs=[ANYV] * len(ins),
        out_specs=[ANYV] * len(outs),
        scratch_shapes=scratch,
        name=name,
        compiler_params=pltpu.CompilerParams(
            collective_id=collective,
            has_side_effects=collective is not None,
            vmem_limit_bytes=LIMIT,
        ),
    )(*ins)


def exchange_kernel(n, *refs):
    count = (len(refs) - 3) // 2
    sources, targets = refs[:count], refs[count : 2 * count]
    send, recv, local = refs[2 * count :]
    dp, me = lax.axis_index("dp"), lax.axis_index("seq")
    barrier = pltpu.get_barrier_semaphore()

    @pl.loop(1, n)
    def _(i):
        pl.semaphore_signal(barrier, inc=1, device_id=(dp, lax.rem(me + i, n)), device_id_type=MESH)

    pl.semaphore_wait(barrier, n - 1)
    own = []
    for j, (source, target) in enumerate(zip(sources, targets)):
        own.append(pltpu.make_async_copy(source.at[me], target.at[me], local.at[j]))
        own[-1].start()

    def copy(j, i, block, slot, to):
        return pltpu.make_async_remote_copy(
            src_ref=sources[j].at[block],
            dst_ref=targets[j].at[slot],
            send_sem=send.at[j, i],
            recv_sem=recv.at[j, i],
            device_id=(dp, to),
            device_id_type=MESH,
        )

    for j in range(count):

        @pl.loop(1, n)
        def _(i):
            to = lax.rem(me + i, n)
            copy(j, i, to, me, to).start()

    for c in own:
        c.wait()
    for j in range(count):

        @pl.loop(1, n)
        def _(i):
            origin = lax.rem(me - i + n, n)
            copy(j, i, origin, origin, origin).wait()


def exchange(arrays, collective):
    return call(
        functools.partial(exchange_kernel, GROUPS),
        arrays,
        [shape(*a.shape) for a in arrays],
        [
            pltpu.SemaphoreType.DMA((len(arrays), GROUPS)),
            pltpu.SemaphoreType.DMA((len(arrays), GROUPS)),
            pltpu.SemaphoreType.DMA((len(arrays),)),
        ],
        "exchange",
        collective,
    )


def at_xyz(x, y, z, core):
    return lax.rem(y, 2) * 2 + core, (x * 8 + z) * 2 + lax.div(y, 2)


def lane_shards(tile, x_first):
    if x_first:
        x, y_hi, z_hi = tile // 4, tile // 2 % 2, tile % 2
    else:
        y_hi, x, z_hi = tile // 8, tile // 2 % 4, tile % 2
    return [(x * 8 + z_hi * 4 + i) * 2 + y_hi for i in range(4)]


def spread(source, base, width, lead, first, count, step, place):
    columns = [place(c) for s in lead for c in (s, s + count - 1)]
    low = min(columns) // 128 * 128
    high = -(-(max(columns) + 1) // 128) * 128
    row = lax.broadcasted_iota(jnp.int32, (high - low, 128), 0) + low
    lane = lax.broadcasted_iota(jnp.int32, (high - low, 128), 1)
    slot, inner = lax.shift_right_logical(lane, 5), (lane & 31) - first
    column = lead[0] + slot * step + inner
    wanted = column + sum(
        jnp.where(column >= edge, gap, 0) for edge, gap in zip(base, width)
    )
    chosen = (row == wanted) & (inner >= 0) & (inner < count)
    return dot(source[:, low:high], chosen.astype(F32).astype(BF16)).astype(BF16)


def gradients(c, x_first, ht, at, ht_far, at_far, dpk, dpk_far, dy, dy_far, mine, far, write):
    edges, gaps = (HD, 2 * HD), (PAD - HD, PAD - HD)

    def place(o):
        return o + (PAD - HD) * (o // HD)

    for chunk in range(4):
        for t in range(4):
            tile = chunk * 4 + t
            shards = lane_shards(tile, x_first)
            at_t = slice(t * 128, (t + 1) * 128)
            for (d, e), out in zip(((dpk, dy), (dpk_far, dy_far)), (mine, far)):
                lead = [27 * s for s in shards]
                out[0, :, at_t] = spread(d, edges, gaps, lead, 0, 27, 54, place)
                lead = [18 * s for s in shards]
                plain = spread(e, (), (), lead, 0, 18, 36, lambda o: o)
                for g in range(2):
                    lead = [18 * s + 9 * g for s in shards]
                    out[1 + 2 * g, :, at_t] = plain
                    out[2 + 2 * g, :, at_t] = spread(e, (), (), lead, 18, 9, 36, lambda o: o)
        for y_lo in range(2):
            block = y_lo * 2 + c
            rows = pl.ds(pl.multiple_of(block * QROWS, 32), QROWS)
            total = dot(ht[rows, :], mine[0]) + dot(ht_far[y_lo], far[0])
            write(chunk, y_lo, 0, QROWS, total)
            for g in range(2):
                near = pl.ds(pl.multiple_of(block * 144 + 48 * g, 16), 48)
                last = pl.ds(pl.multiple_of(block * 144 + 96, 16), 48)
                total = dot(at[near, :], mine[1 + 2 * g]) + dot(at[last, :], mine[2 + 2 * g])
                total += dot(at_far[y_lo, 48 * g : 48 * g + 48, :], far[1 + 2 * g])
                total += dot(at_far[y_lo, 96:144, :], far[2 + 2 * g])
                write(chunk, y_lo, QROWS + 48 * g, 48, total)


def reduce_kernel(*refs):
    (
        ht_s, at_s, dpk_s, dy_s, ht_t, at_t, dpk_t, dy_t,
        out,
        hf, af, df, yf, mine, far,
        g_s, g_t, r1_s, r1_t, r2_s, r2_t,
        h_s, h_t, r3_s, r3_t, r4_s, r4_t,
        zs, zr, send, recv,
    ) = refs
    dp, me = lax.axis_index("dp"), lax.axis_index("seq")
    core, y_lo = lax.rem(dp, 2), lax.div(dp, 2)
    y_hi, z, x = lax.rem(me, 2), lax.rem(lax.div(me, 2), 8), lax.div(me, 16)
    y = y_hi * 2 + y_lo
    pair = at_xyz(x, y, z, 1 - core)

    def along_x(k):
        return at_xyz(lax.rem(x + k, 4), y, z, core)

    def along_y(k):
        return at_xyz(x, lax.rem(y + k, 4), z, core)

    def along_z(k):
        return at_xyz(x, y, lax.rem(z + k, 8), core)

    barrier = pltpu.get_barrier_semaphore()
    friends = [pair] + [along_x(1), along_x(3), along_y(1), along_y(3)]
    friends += [along_z(k) for k in range(1, 8)]
    for friend in friends:
        pl.semaphore_signal(barrier, inc=1, device_id=friend, device_id_type=MESH)
    pl.semaphore_wait(barrier, len(friends))

    used = [0]

    def copy(source, target, to):
        i = used[0]
        used[0] += 1
        c = pltpu.make_async_remote_copy(
            src_ref=source,
            dst_ref=target,
            send_sem=send.at[i],
            recv_sem=recv.at[i],
            device_id=to,
            device_id_type=MESH,
        )
        c.start()
        return c

    landed = []
    for b, (ht, at, dpk, dy) in enumerate(((ht_s, at_s, dpk_s, dy_s), (ht_t, at_t, dpk_t, dy_t))):
        copies = [copy(dpk, df.at[b], pair), copy(dy, yf.at[b], pair)]
        for i in range(2):
            block = i * 2 + 1 - core
            rows = pl.ds(pl.multiple_of(block * QROWS, 32), QROWS)
            copies.append(copy(ht.at[rows, :], hf.at[b, i], pair))
            rows = pl.ds(pl.multiple_of(block * 144, 16), 144)
            copies.append(copy(at.at[rows, :], af.at[b, i], pair))
        landed.append(copies)

    def write_s(chunk, y_lo, row, count, value):
        g_s[chunk, pl.ds(y_lo * ROWS + row, count), :] = value.astype(BF16)

    def write_t(chunk, y_lo, row, count, value):
        half = slice(chunk % 2 * 512, (chunk % 2 + 1) * 512)
        g_t[chunk // 2 * 2 + y_lo, pl.ds(row, count), half] = value.astype(BF16)

    def first(g, relay, near, place, along):
        rows = g.shape[1] // 2
        two, up, down = lax.rem(place + 2, 4), lax.rem(place + 1, 4), lax.rem(place + 3, 4)
        top, bottom = pl.ds(0, rows), pl.ds(rows, rows)
        return [
            copy(g.at[two, top], relay.at[0], along(1)),
            copy(g.at[two, bottom], relay.at[1], along(3)),
            copy(g.at[up, bottom], near.at[0, bottom], along(1)),
            copy(g.at[down, top], near.at[1, top], along(3)),
        ]

    def second(g, relay, near, place, along, started):
        rows = g.shape[1] // 2
        up, down = lax.rem(place + 1, 4), lax.rem(place + 3, 4)
        top, bottom = pl.ds(0, rows), pl.ds(rows, rows)
        started[0].wait()
        g[up, top] = (g[up, top].astype(F32) + relay[0].astype(F32)).astype(BF16)
        a = copy(g.at[up, top], near.at[0, top], along(1))
        started[1].wait()
        g[down, bottom] = (g[down, bottom].astype(F32) + relay[1].astype(F32)).astype(BF16)
        b = copy(g.at[down, bottom], near.at[1, bottom], along(3))
        return [started[2], started[3], a, b]

    def total(g, near, place, started):
        for c in started:
            c.wait()
        return g[place].astype(F32) + near[0].astype(F32) + near[1].astype(F32)

    for c in landed[0]:
        c.wait()
    gradients(core, True, ht_s, at_s, hf.at[0], af.at[0], dpk_s, df.at[0], dy_s, yf.at[0], mine, far, write_s)
    s1 = first(g_s, r1_s, r2_s, x, along_x)
    for c in landed[1]:
        c.wait()
    gradients(core, False, ht_t, at_t, hf.at[1], af.at[1], dpk_t, df.at[1], dy_t, yf.at[1], mine, far, write_t)
    t1 = first(g_t, r1_t, r2_t, y, along_y)
    s1 = second(g_s, r1_s, r2_s, x, along_x, s1)
    t1 = second(g_t, r1_t, r2_t, y, along_y, t1)

    sum_s = total(g_s, r2_s, x, s1).astype(BF16)
    for i in range(2):
        for j in range(2):
            h_s[j * 2 + i] = sum_s[i * ROWS : (i + 1) * ROWS, j * 256 : (j + 1) * 256]
    s2 = first(h_s, r3_s, r4_s, y, along_y)
    sum_t = total(g_t, r2_t, y, t1).astype(BF16)
    for i in range(4):
        h_t[i] = sum_t[:, i * 256 : (i + 1) * 256]
    t2 = first(h_t, r3_t, r4_t, x, along_x)
    s2 = second(h_s, r3_s, r4_s, y, along_y, s2)
    t2 = second(h_t, r3_t, r4_t, x, along_x, t2)
    copies = []
    for b, (h, near, place, started) in enumerate(((h_s, r4_s, y, s2), (h_t, r4_t, x, t2))):
        zs[b] = total(h, near, place, started).T.reshape(8, 32, ROWS).astype(BF16)
        for k in range(1, 8):
            to = lax.rem(z + k, 8)
            copies.append(copy(zs.at[b, to], zr.at[b, k], along_z(k)))
    for b in range(2):
        acc = zs[b, z].astype(F32)
        for k in range(1, 8):
            copies[b * 7 + k - 1].wait()
            acc = acc + zr[b, k].astype(F32)
        out[b] = acc


def reduce_grads(space, time, collective):
    copies = 12 + 4 * 6 + 14
    return call(
        reduce_kernel,
        [*space, *time],
        [shape(2, 32, ROWS, dtype=F32)],
        [
            VMEM((2, 2, QROWS, TOK), BF16),
            VMEM((2, 2, 144, TOK), BF16),
            VMEM((2, TOK, 3 * PAD), BF16),
            VMEM((2, TOK, D), BF16),
            VMEM((5, TOK, 512), BF16),
            VMEM((5, TOK, 512), BF16),
            VMEM((4, 2 * ROWS, 512), BF16),
            VMEM((4, ROWS, 1024), BF16),
            VMEM((2, ROWS, 512), BF16),
            VMEM((2, ROWS // 2, 1024), BF16),
            VMEM((2, 2 * ROWS, 512), BF16),
            VMEM((2, ROWS, 1024), BF16),
            VMEM((4, ROWS, 256), BF16),
            VMEM((4, ROWS, 256), BF16),
            VMEM((2, ROWS // 2, 256), BF16),
            VMEM((2, ROWS // 2, 256), BF16),
            VMEM((2, ROWS, 256), BF16),
            VMEM((2, ROWS, 256), BF16),
            VMEM((2, 8, 32, ROWS), BF16),
            VMEM((2, 8, 32, ROWS), BF16),
            pltpu.SemaphoreType.DMA((copies,)),
            pltpu.SemaphoreType.DMA((copies,)),
        ],
        "reduce_grads",
        collective,
    )[0]


def own_rows(block):
    qkv = block[:27, :QROWS]
    tail = block[18:27, QROWS:]
    left = block[:18, QROWS:]
    right = jnp.concatenate([tail[:, :48], tail[:, 48:]], axis=0)
    return qkv, jnp.concatenate([left, right], axis=1)


def per_device(latents, out_grad, qkv_spatial, proj_spatial, qkv_temporal, proj_temporal):
    x, dy = latents[0, 0], out_grad[0, 0]
    blocks = shape(GROUPS, D // 128, OWN, 128)
    wide, narrow = shape(TOK, D), shape(TOK, PAD)
    acc = VMEM((TOK, PAD), F32)
    factors = [wide, shape(D, TOK), shape(PAD, TOK), shape(TOK, 3 * PAD)]
    nxt, dyb, q, k, v, attn = call(
        space_forward,
        [x, dy, qkv_spatial, proj_spatial],
        [blocks, blocks, narrow, narrow, narrow, narrow],
        [acc],
        "space_forward",
    )
    nxt, dyb = exchange([nxt, dyb], 0)
    narrows = [VMEM((TOK, PAD), BF16)] * 5
    dxb, dy_t, ht_t, at_t, dpk_t = call(
        time_both,
        [nxt, dyb, qkv_temporal, proj_temporal],
        [blocks, *factors],
        [*narrows, acc, acc, acc],
        "time_both",
    )
    (dxb,) = exchange([dxb], 1)
    dx, dy_s, ht_s, at_s, dpk_s = call(
        space_back,
        [x, dxb, qkv_spatial, proj_spatial, q, k, v, attn],
        [wide, *factors],
        [narrows[0], acc, acc, acc],
        "space_back",
    )
    sums = reduce_grads((ht_s, at_s, dpk_s, dy_s), (ht_t, at_t, dpk_t, dy_t), 2)
    qkv_s, proj_s = own_rows(sums[0])
    qkv_t, proj_t = own_rows(sums[1])
    return dx[None, None], qkv_s, proj_s, qkv_t, proj_t


def solution(mesh):
    placed = (P("dp", "seq", None, None), P("dp", "seq", None, None), P(), P(), P(), P())
    return jax.shard_map(
        per_device,
        mesh=mesh,
        in_specs=placed,
        out_specs=(
            P("dp", "seq", None, None),
            P("seq", "dp"),
            P("seq", "dp"),
            P("seq", "dp"),
            P("seq", "dp"),
        ),
        check_vma=False,
    )
```

```python
import jax
import jax.numpy as jnp
from jax import lax
from jax.experimental import pallas as pl
from jax.experimental.pallas import tpu as pltpu
from jax.sharding import PartitionSpec as P

HDIM = 72
HEADS = 8
HD = HDIM * HEADS
PAD = 640
D = 1152
TOK = 256
GROUPS = 64
OWN = TOK // GROUPS
EPS = 1e-06
SCALE = HDIM ** (-0.5)
NEG = -1e30
MESH = pl.DeviceIdType.MESH
VMEM = pltpu.VMEM
F32 = jnp.float32
BF16 = jnp.bfloat16
LIMIT = 60 * 2**20

QROWS = 288
PROWS = 96
ROWS = QROWS + PROWS
PART = ROWS // 2
TILES = 16
QWIN = 384
PWIN = 256


def dot(a, b, dims=((1,), (0,))):
    return lax.dot_general(a, b, (dims, ((), ())), preferred_element_type=F32)


NT = ((1,), (1,))
TN = ((0,), (0,))


def window(head):
    low = head * HDIM // 128 * 128
    return low, -(-(head + 1) * HDIM // 128) * 128


def head_mask(head, low, high):
    lane = lax.broadcasted_iota(jnp.int32, (1, high - low), 1) + low
    return ((lane >= head * HDIM) & (lane < (head + 1) * HDIM)).astype(F32).astype(BF16)


def normalize(x):
    inverse = lax.rsqrt(jnp.mean(x * x, axis=-1, keepdims=True) + EPS)
    return x * inverse, inverse


def project(hidden, w_ref, targets):
    for i, target in enumerate(targets):
        target[:, :HD] = dot(hidden, w_ref[i * HD : (i + 1) * HD, :], NT).astype(BF16)
        target[:, HD:] = jnp.zeros((TOK, PAD - HD), BF16)


def softmax(qm, k, keep):
    s = dot(qm, k, NT) * SCALE
    if keep is not None:
        s = jnp.where(keep, s, NEG)
    e = jnp.exp(s - jnp.max(s, axis=-1, keepdims=True))
    return e * (1.0 / jnp.sum(e, axis=-1, keepdims=True))


def same_position():
    rows = lax.broadcasted_iota(jnp.int32, (TOK, TOK), 0)
    columns = lax.broadcasted_iota(jnp.int32, (TOK, TOK), 1)
    return lax.rem(rows, OWN) == lax.rem(columns, OWN)


def attention(q, k, v, acc, attn, keep):
    acc[...] = jnp.zeros_like(acc)
    for h in range(HEADS):
        low, high = window(h)
        mask = head_mask(h, low, high)
        probs = softmax(q[:, low:high] * mask, k[:, low:high], keep)
        acc[:, low:high] += dot(probs.astype(BF16), v[:, low:high] * mask)
    attn[...] = acc[...].astype(BF16)


def attention_back(q, k, v, attn, da, accs, keep, hooks):
    for acc in accs:
        acc[...] = jnp.zeros_like(acc)
    dq, dk, dv = accs
    for h in range(HEADS):
        if h in hooks:
            hooks[h]()
        low, high = window(h)
        mask = head_mask(h, low, high)
        qm = q[:, low:high] * mask
        km = k[:, low:high] * mask
        dam = da[:, low:high] * mask
        probs = softmax(qm, k[:, low:high], keep)
        d_probs = dot(dam, v[:, low:high], NT)
        dv[:, low:high] += dot(probs.astype(BF16), dam, TN)
        offset = jnp.sum(dam.astype(F32) * attn[:, low:high].astype(F32), axis=-1, keepdims=True)
        ds = (probs * (d_probs - offset) * SCALE).astype(BF16)
        dq[:, low:high] += dot(ds, km)
        dk[:, low:high] += dot(ds, qm, TN)


def pack(accs, dpk):
    for i, acc in enumerate(accs):
        dpk[:, i * PAD : (i + 1) * PAD] = acc[...].astype(BF16)


def block_back(dy, x, w_ref, dpk):
    d_hidden = jnp.zeros((TOK, D), F32)
    for i in range(3):
        part = dpk[:, i * PAD : i * PAD + HD]
        d_hidden = d_hidden + dot(part, w_ref[i * HD : (i + 1) * HD, :])
    normed, inverse = normalize(x)
    along = jnp.mean(d_hidden * normed, axis=-1, keepdims=True)
    return dy.astype(F32) + inverse * (d_hidden - normed * along)


def to_blocks(value, ref):
    for t in range(D // 128):
        ref[:, t, :, :] = value[:, t * 128 : (t + 1) * 128].reshape(GROUPS, OWN, 128)


def from_blocks(ref):
    return jnp.concatenate([ref[:, t, :, :].reshape(TOK, 128) for t in range(D // 128)], axis=1)


def at_xyz(x, y, z, core):
    return lax.rem(y, 2) * 2 + core, (x * 8 + z) * 2 + lax.div(y, 2)


def lane_shards(tile):
    x, y_hi, z_hi = tile // 4, tile // 2 % 2, tile % 2
    return [(x * 8 + z_hi * 4 + i) * 2 + y_hi for i in range(4)]


def qplace(column):
    return column + (PAD - HD) * (column // HD)


def qlow(tile):
    return min(qplace(27 * lane_shards(tile)[0]) // 128 * 128, 3 * PAD - QWIN)


def plow(tile):
    return min(18 * lane_shards(tile)[0] // 128 * 128, D - PWIN)


def choice(low, window, lead, first, count, step, edges):
    row = lax.broadcasted_iota(jnp.int32, (window, 128), 0) + low
    lane = lax.broadcasted_iota(jnp.int32, (1, 128), 1)
    inner = (lane & 31) - first
    wanted = lead + lax.shift_right_logical(lane, 5) * step + inner
    gaps = sum((jnp.where(wanted >= e, PAD - HD, 0) for e in edges), jnp.zeros_like(wanted))
    wanted = jnp.where((inner >= 0) & (inner < count), wanted + gaps, -1)
    return (row == wanted).astype(F32).astype(BF16)


def spreaders(qs, ps):
    for tile in range(TILES):
        shard = lane_shards(tile)[0]
        qs[tile] = choice(qlow(tile), QWIN, 27 * shard, 0, 27, 54, (HD, 2 * HD))
        low = plow(tile)
        ps[tile, :, 0:128] = choice(low, PWIN, 18 * shard, 0, 18, 36, ())
        ps[tile, :, 128:256] = choice(low, PWIN, 18 * shard, 18, 9, 36, ())
        ps[tile, :, 256:384] = choice(low, PWIN, 18 * shard + 9, 18, 9, 36, ())


def gradients(qs, ps, hcat, a01, a2, dpk, dy, mq, mp, ga, gb):
    for x in range(4):
        for t in range(4):
            tile, here = x * 4 + t, slice(t * 128, (t + 1) * 128)
            low = qlow(tile)
            mq[:, here] = dot(dpk[:, low : low + QWIN], qs[tile]).astype(BF16)
            low = plow(tile)
            spread = dot(dy[:, low : low + PWIN], ps[tile]).astype(BF16)
            for j in range(3):
                mp[j, :, here] = spread[:, j * 128 : (j + 1) * 128]
        qkv = dot(hcat[...], mq[...])
        proj = dot(a01[...], mp[0])
        last = [dot(a2[...], mp[1]), dot(a2[...], mp[2])]
        for y_lo in range(2):
            for y_hi in range(2):
                here = slice(y_hi * 256, (y_hi + 1) * 256)
                row = y_lo * QROWS
                ga[x, y_hi, y_lo] = qkv[row : row + PART, here].astype(BF16)
                gb[x, y_hi, y_lo, 0:96] = qkv[row + PART : row + QROWS, here].astype(BF16)
                for g in range(2):
                    both = proj[y_lo * 96 + g * 48 : y_lo * 96 + g * 48 + 48, here]
                    both = both + last[g][y_lo * 48 : y_lo * 48 + 48, here]
                    gb[x, y_hi, y_lo, 96 + 48 * g : 144 + 48 * g] = both.astype(BF16)


class Ring:
    def __init__(self, copy, block, relay, near, place, along):
        self.copy, self.block, self.relay, self.near = copy, block, relay, near
        self.up, self.down = lax.rem(place + 1, 4), lax.rem(place + 3, 4)
        self.two = lax.rem(place + 2, 4)
        self.to_up, self.to_down = along(1), along(3)

    def first(self):
        copy, block, near = self.copy, self.block, self.near
        self.on_way = (
            copy(block(self.two, 0), self.relay.at[0], self.to_up),
            copy(block(self.two, 1), self.relay.at[1], self.to_down),
        )
        self.copies = [
            copy(block(self.up, 1), near.at[0, 1], self.to_up),
            copy(block(self.down, 0), near.at[1, 0], self.to_down),
        ]

    def second(self):
        copy, block, near = self.copy, self.block, self.near
        steps = ((self.up, 0, self.to_up), (self.down, 1, self.to_down))
        for side, (place, half, to) in enumerate(steps):
            self.on_way[side].wait()
            ref = block(place, half)
            ref[...] = (ref[...].astype(F32) + self.relay[side].astype(F32)).astype(BF16)
            self.copies.append(copy(ref, near.at[side, half], to))

    def total(self, own):
        for c in self.copies:
            c.wait()
        near = self.near[0].astype(F32) + self.near[1].astype(F32)
        return own.astype(F32) + near.reshape(own.shape)


def kernel(
    x_in, dy_in, ws_in, ps_in, wt_in, pt_in,
    dx_out, gqs, gps, gqt, gpt,
    x_v, dy_v, ws, ps, wt, pt,
    dyb, dyr, nxb, nxr, dxb, dxr,
    qs, ks, vs, os, qt, kt, vt, ot, da, acc0, acc1, acc2,
    ht, at, hcat, a01, a2, dpk, dyf,
    spread_q, spread_p, mq, mp,
    ga, gb, relay_a, relay_b, near_a, near_b,
    ha, hb, relay2_a, relay2_b, near2_a, near2_b,
    zs, zr,
    send, recv, all_send, all_recv, local,
):
    dp, me = lax.axis_index("dp"), lax.axis_index("seq")
    core, y_lo = lax.rem(dp, 2), lax.div(dp, 2)
    y_hi, z, x = lax.rem(me, 2), lax.rem(lax.div(me, 2), 8), lax.div(me, 16)
    y = y_hi * 2 + y_lo
    n = GROUPS
    pair = at_xyz(x, y, z, 1 - core)

    def along_x(k):
        return at_xyz(lax.rem(x + k, 4), y, z, core)

    def along_y(k):
        return at_xyz(x, lax.rem(y + k, 4), z, core)

    def along_z(k):
        return at_xyz(x, y, lax.rem(z + k, 8), core)

    counts = [0, 0]

    def here(source, target):
        c = pltpu.make_async_copy(source, target, local.at[counts[0]])
        counts[0] += 1
        c.start()
        return c

    def copy(source, target, to):
        i = counts[1]
        counts[1] += 1
        c = pltpu.make_async_remote_copy(
            src_ref=source,
            dst_ref=target,
            send_sem=send.at[i],
            recv_sem=recv.at[i],
            device_id=to,
            device_id_type=MESH,
        )
        c.start()
        return c

    get_dy = here(dy_in, dy_v)
    get_x = here(x_in, x_v)
    get_ws = here(ws_in, ws)
    get_ps = here(ps_in, ps)
    get_wt = here(wt_in, wt)
    get_pt = here(pt_in, pt)

    barrier = pltpu.get_barrier_semaphore()

    @pl.loop(1, n)
    def _(i):
        pl.semaphore_signal(barrier, inc=1, device_id=(dp, lax.rem(me + i, n)), device_id_type=MESH)

    for friend in (pair, along_y(1), along_y(3)):
        pl.semaphore_signal(barrier, inc=1, device_id=friend, device_id_type=MESH)

    def exchange_start(j, source, target):
        @pl.loop(1, n)
        def _(i):
            to = lax.rem(me + i, n)
            pltpu.make_async_remote_copy(
                src_ref=source.at[to],
                dst_ref=target.at[me],
                send_sem=all_send.at[j],
                recv_sem=all_recv.at[j],
                device_id=(dp, to),
                device_id_type=MESH,
            ).start()

        return here(source.at[me], target.at[me])

    def exchange_wait(j, source, target, own):
        own.wait()
        pltpu.make_async_remote_copy(
            src_ref=source.at[pl.ds(0, n - 1)],
            dst_ref=target.at[pl.ds(0, n - 1)],
            send_sem=all_send.at[j],
            recv_sem=all_recv.at[j],
            device_id=pair,
            device_id_type=MESH,
        ).wait()

    far = pl.ds(TOK, TOK)

    def share_forward(b):
        copies = []
        for i in range(2):
            block = i * 2 + 1 - core
            rows = pl.ds(pl.multiple_of(block * QROWS, 32), QROWS)
            copies.append(copy(ht.at[b, rows], hcat.at[b, pl.ds(i * QROWS, QROWS), far], pair))
            rows = pl.ds(pl.multiple_of(block * 144, 16), 96)
            copies.append(copy(at.at[b, rows], a01.at[b, pl.ds(i * 96, 96), far], pair))
            rows = pl.ds(pl.multiple_of(block * 144 + 96, 16), 48)
            copies.append(copy(at.at[b, rows], a2.at[b, pl.ds(i * 48, 48), far], pair))
            block = i * 2 + core
            rows = pl.ds(pl.multiple_of(block * QROWS, 32), QROWS)
            hcat[b, i * QROWS : (i + 1) * QROWS, :TOK] = ht[b, rows, :]
            rows = pl.ds(pl.multiple_of(block * 144, 16), 96)
            a01[b, i * 96 : (i + 1) * 96, :TOK] = at[b, rows, :]
            rows = pl.ds(pl.multiple_of(block * 144 + 96, 16), 48)
            a2[b, i * 48 : (i + 1) * 48, :TOK] = at[b, rows, :]
        return copies

    def share(ref, b):
        return copy(ref.at[b, pl.ds(0, TOK)], ref.at[b, far], pair)

    def rings(b):
        first = (
            Ring(copy, lambda i, h: ga.at[b, i, h], relay_a.at[b], near_a.at[b], x, along_x),
            Ring(
                copy,
                lambda i, h: gb.at[b, pl.ds(2 * h, 2), lax.div(i, 2), lax.rem(i, 2)],
                relay_b.at[b], near_b.at[b], y, along_y,
            ),
        )
        half = PART // 2
        second = (
            Ring(copy, lambda i, h: ha.at[b, i, pl.ds(h * half, half)], relay2_a.at[b], near2_a.at[b], y, along_y),
            Ring(copy, lambda i, h: hb.at[b, i, pl.ds(h * half, half)], relay2_b.at[b], near2_b.at[b], x, along_x),
        )
        return first, second

    def weight_terms(b, copies):
        for c in copies:
            c.wait()
        gradients(
            spread_q, spread_p, hcat.at[b], a01.at[b], a2.at[b], dpk.at[b], dyf.at[b], mq, mp, ga.at[b], gb.at[b]
        )

    def between(b, first, second):
        ha[b] = first[0].total(ga[b, x].reshape(4, PART, 256)).astype(BF16)
        second[0].first()
        hb[b] = first[1].total(gb[b, :, y_hi, y_lo]).astype(BF16)
        second[1].first()

    def last(b, second):
        sums = [second[0].total(ha[b, y]), second[1].total(hb[b, x])]
        sums = jnp.concatenate(sums, axis=0).T
        zs[b] = sums.reshape(8, 32, ROWS).astype(BF16)
        copies = []
        for k in range(1, 8):
            copies.append(copy(zs.at[b, lax.rem(z + k, 8)], zr.at[b, k], along_z(k)))
        return copies

    def finish(b, copies, qkv, proj):
        acc = zs[b, z].astype(F32)
        for k in range(1, 8):
            copies[k - 1].wait()
            acc = acc + zr[b, k].astype(F32)
        qkv[...] = acc[:27, :QROWS]
        proj[:, 0:96] = acc[:18, QROWS:]
        proj[0:9, 96:144] = acc[18:27, QROWS : QROWS + 48]
        proj[9:18, 96:144] = acc[18:27, QROWS + 48 :]

    SPACE, TIME = 0, 1

    get_dy.wait()
    to_blocks(dy_v[...], dyb)
    pl.semaphore_wait(barrier, n + 2)
    own_dy = exchange_start(0, dyb, dyr)
    get_x.wait()
    source = x_v[...].astype(F32)
    normed, _ = normalize(source)
    hidden = normed.astype(BF16)
    get_ws.wait()
    project(hidden, ws, (qs, ks, vs))
    attention(qs, ks, vs, acc0, os, None)
    get_ps.wait()
    to_blocks((source + dot(os[:, :HD], ps[...])).astype(BF16), nxb)
    own_next = exchange_start(1, nxb, nxr)
    ht[SPACE] = hidden.T
    at[SPACE] = os[...].T
    shared_s = share_forward(SPACE)
    spreaders(spread_q, spread_p)

    get_wt.wait()
    get_pt.wait()
    exchange_wait(1, nxb, nxr, own_next)
    middle = from_blocks(nxr)
    normed, _ = normalize(middle.astype(F32))
    hidden = normed.astype(BF16)
    ht[TIME] = hidden.T
    project(hidden, wt, (qt, kt, vt))
    keep = same_position()
    attention(qt, kt, vt, acc0, ot, keep)
    at[TIME] = ot[...].T
    shared_t = share_forward(TIME)
    exchange_wait(0, dyb, dyr, own_dy)
    dy = from_blocks(dyr)
    dyf[TIME, :TOK, :] = dy
    shared_t.append(share(dyf, TIME))
    da[:, :HD] = dot(dy, pt[...], NT).astype(BF16)
    da[:, HD:] = jnp.zeros((TOK, PAD - HD), BF16)
    accs = (acc0, acc1, acc2)
    attention_back(qt, kt, vt, ot, da, accs, keep, {})
    pack(accs, dpk.at[TIME, pl.ds(0, TOK)])
    shared_t.append(share(dpk, TIME))
    middle = from_blocks(nxr).astype(F32)
    to_blocks(block_back(dy, middle, wt, dpk.at[TIME, pl.ds(0, TOK)]).astype(BF16), dxb)
    own_dx = exchange_start(2, dxb, dxr)

    first_t, second_t = rings(TIME)
    weight_terms(TIME, shared_t)
    for r in first_t:
        r.first()

    exchange_wait(2, dxb, dxr, own_dx)
    dy = from_blocks(dxr)
    dyf[SPACE, :TOK, :] = dy
    shared_s.append(share(dyf, SPACE))
    da[:, :HD] = dot(dy, ps[...], NT).astype(BF16)

    def hook_second():
        for r in first_t:
            r.second()

    def hook_between():
        between(TIME, first_t, second_t)

    attention_back(qs, ks, vs, os, da, accs, None, {0: hook_second, 5: hook_between})
    pack(accs, dpk.at[SPACE, pl.ds(0, TOK)])
    shared_s.append(share(dpk, SPACE))
    for r in second_t:
        r.second()
    dx_out[...] = block_back(dy, x_v[...].astype(F32), ws, dpk.at[SPACE, pl.ds(0, TOK)]).astype(BF16)
    first_s, second_s = rings(SPACE)
    weight_terms(SPACE, shared_s)
    for r in first_s:
        r.first()
    along = last(TIME, second_t)
    for r in first_s:
        r.second()
    finish(TIME, along, gqt, gpt)
    between(SPACE, first_s, second_s)
    for r in second_s:
        r.second()
    finish(SPACE, last(SPACE, second_s), gqs, gps)


def per_device(latents, out_grad, qkv_spatial, proj_spatial, qkv_temporal, proj_temporal):
    ins = [latents[0, 0], out_grad[0, 0], qkv_spatial, proj_spatial.T, qkv_temporal, proj_temporal.T]
    wide, narrow = VMEM((TOK, D), BF16), VMEM((TOK, PAD), BF16)
    qkv, proj = VMEM((3 * HD, D), BF16), VMEM((HD, D), BF16)
    blocks = VMEM((GROUPS, D // 128, OWN, 128), BF16)
    acc = VMEM((TOK, PAD), F32)
    terms = VMEM((2, 4, 2, 2, PART, 256), BF16)
    half = PART // 2
    dma = pltpu.SemaphoreType.DMA
    f32 = [jax.ShapeDtypeStruct(s, F32) for s in ((27, 288), (18, 144), (27, 288), (18, 144))]
    outs = [jax.ShapeDtypeStruct((TOK, D), BF16), *f32]
    dx, qkv_s, proj_s, qkv_t, proj_t = pl.pallas_call(
        kernel,
        out_shape=outs,
        in_specs=[pl.BlockSpec(memory_space=pl.ANY)] * len(ins),
        out_specs=[pl.BlockSpec(memory_space=VMEM)] * len(outs),
        scratch_shapes=[
            wide, wide, qkv, proj, qkv, proj,
            *[blocks] * 6,
            *[narrow] * 9, acc, acc, acc,
            VMEM((2, D, TOK), BF16),
            VMEM((2, PAD, TOK), BF16),
            VMEM((2, 2 * QROWS, 2 * TOK), BF16),
            VMEM((2, 192, 2 * TOK), BF16),
            VMEM((2, 96, 2 * TOK), BF16),
            VMEM((2, 2 * TOK, 3 * PAD), BF16),
            VMEM((2, 2 * TOK, D), BF16),
            VMEM((TILES, QWIN, 128), BF16),
            VMEM((TILES, PWIN, 384), BF16),
            VMEM((2 * TOK, 512), BF16),
            VMEM((3, 2 * TOK, 512), BF16),
            terms, terms,
            *[VMEM((2, 2, 2, PART, 256), BF16)] * 2,
            *[VMEM((2, 2, 2, 2, PART, 256), BF16)] * 2,
            *[VMEM((2, 4, PART, 256), BF16)] * 2,
            *[VMEM((2, 2, half, 256), BF16)] * 2,
            *[VMEM((2, 2, 2, half, 256), BF16)] * 2,
            *[VMEM((2, 8, 32, ROWS), BF16)] * 2,
            dma((78,)), dma((78,)), dma((3,)), dma((3,)), dma((9,)),
        ],
        name="both_blocks",
        compiler_params=pltpu.CompilerParams(
            collective_id=0, has_side_effects=True, vmem_limit_bytes=LIMIT
        ),
    )(*ins)
    return dx[None, None], qkv_s, proj_s, qkv_t, proj_t


def solution(mesh):
    placed = (P("dp", "seq", None, None), P("dp", "seq", None, None), P(), P(), P(), P())
    return jax.shard_map(
        per_device,
        mesh=mesh,
        in_specs=placed,
        out_specs=(
            P("dp", "seq", None, None),
            P("seq", "dp"),
            P("seq", "dp"),
            P("seq", "dp"),
            P("seq", "dp"),
        ),
        check_vma=False,
    )
```

```python
import jax
import jax.numpy as jnp
from jax import lax
from jax.experimental import pallas as pl
from jax.experimental.pallas import tpu as pltpu
from jax.sharding import PartitionSpec as P

HDIM = 72
HEADS = 8
HD = HDIM * HEADS
PAD = 640
D = 1152
TOK = 256
GROUPS = 64
OWN = TOK // GROUPS
EPS = 1e-06
SCALE = HDIM ** (-0.5)
NEG = -1e30
MESH = pl.DeviceIdType.MESH
VMEM = pltpu.VMEM
F32 = jnp.float32
BF16 = jnp.bfloat16
LIMIT = 60 * 2**20

QROWS = 288
PROWS = 96
ROWS = QROWS + PROWS
PARTS = ((144, True), (144, False), (48, True), (48, False))
TILES = 16
QWIN = 384
PWIN = 256


def dot(a, b, dims=((1,), (0,))):
    return lax.dot_general(a, b, (dims, ((), ())), preferred_element_type=F32)


NT = ((1,), (1,))
TN = ((0,), (0,))


def window(head):
    low = head * HDIM // 128 * 128
    return low, -(-(head + 1) * HDIM // 128) * 128


def head_mask(head, low, high):
    lane = lax.broadcasted_iota(jnp.int32, (1, high - low), 1) + low
    return ((lane >= head * HDIM) & (lane < (head + 1) * HDIM)).astype(F32).astype(BF16)


def normalize(x):
    inverse = lax.rsqrt(jnp.mean(x * x, axis=-1, keepdims=True) + EPS)
    return x * inverse, inverse


def project(hidden, w_ref, targets):
    for i, target in enumerate(targets):
        target[:, :HD] = dot(hidden, w_ref[i * HD : (i + 1) * HD, :], NT).astype(BF16)
        target[:, HD:] = jnp.zeros((TOK, PAD - HD), BF16)


def softmax(qm, k, keep):
    s = dot(qm, k, NT) * SCALE
    if keep is not None:
        s = jnp.where(keep, s, NEG)
    e = jnp.exp(s - jnp.max(s, axis=-1, keepdims=True))
    return e * (1.0 / jnp.sum(e, axis=-1, keepdims=True))


def same_position():
    rows = lax.broadcasted_iota(jnp.int32, (TOK, TOK), 0)
    columns = lax.broadcasted_iota(jnp.int32, (TOK, TOK), 1)
    return lax.rem(rows, OWN) == lax.rem(columns, OWN)


def attention(q, k, v, acc, attn, keep):
    acc[...] = jnp.zeros_like(acc)
    for h in range(HEADS):
        low, high = window(h)
        mask = head_mask(h, low, high)
        probs = softmax(q[:, low:high] * mask, k[:, low:high], keep)
        acc[:, low:high] += dot(probs.astype(BF16), v[:, low:high] * mask)
    attn[...] = acc[...].astype(BF16)


def attention_back(q, k, v, attn, da, accs, keep, hooks):
    for acc in accs:
        acc[...] = jnp.zeros_like(acc)
    dq, dk, dv = accs
    for h in range(HEADS):
        if h in hooks:
            hooks[h]()
        low, high = window(h)
        mask = head_mask(h, low, high)
        qm = q[:, low:high] * mask
        km = k[:, low:high] * mask
        dam = da[:, low:high] * mask
        probs = softmax(qm, k[:, low:high], keep)
        d_probs = dot(dam, v[:, low:high], NT)
        dv[:, low:high] += dot(probs.astype(BF16), dam, TN)
        offset = jnp.sum(dam.astype(F32) * attn[:, low:high].astype(F32), axis=-1, keepdims=True)
        ds = (probs * (d_probs - offset) * SCALE).astype(BF16)
        dq[:, low:high] += dot(ds, km)
        dk[:, low:high] += dot(ds, qm, TN)


def pack(accs, dpk):
    for i, acc in enumerate(accs):
        dpk[:, i * PAD : (i + 1) * PAD] = acc[...].astype(BF16)


def block_back(x, w_ref, dpk):
    d_hidden = jnp.zeros((TOK, D), F32)
    for i in range(3):
        part = dpk[:, i * PAD : i * PAD + HD]
        d_hidden = d_hidden + dot(part, w_ref[i * HD : (i + 1) * HD, :])
    normed, inverse = normalize(x)
    along = jnp.mean(d_hidden * normed, axis=-1, keepdims=True)
    return inverse * (d_hidden - normed * along)


def to_blocks(value, ref):
    for t in range(ref.shape[1]):
        ref[:, t, :, :] = value[:, t * 128 : (t + 1) * 128].reshape(GROUPS, OWN, 128)


def from_blocks(ref):
    return jnp.concatenate([ref[:, t, :, :].reshape(TOK, 128) for t in range(ref.shape[1])], axis=1)


def at_xyz(x, y, z, core):
    return lax.rem(y, 2) * 2 + core, (x * 8 + z) * 2 + lax.div(y, 2)


def lane_shards(tile):
    x, y_hi, z_hi = tile // 4, tile // 2 % 2, tile % 2
    return [(x * 8 + z_hi * 4 + i) * 2 + y_hi for i in range(4)]


def qplace(column):
    return column + (PAD - HD) * (column // HD)


def qlow(tile):
    return min(qplace(27 * lane_shards(tile)[0]) // 128 * 128, 3 * PAD - QWIN)


def plow(tile):
    return min(18 * lane_shards(tile)[0] // 128 * 128, D - PWIN)


def choice(low, window, lead, first, count, step, edges):
    row = lax.broadcasted_iota(jnp.int32, (window, 128), 0) + low
    lane = lax.broadcasted_iota(jnp.int32, (1, 128), 1)
    inner = (lane & 31) - first
    wanted = lead + lax.shift_right_logical(lane, 5) * step + inner
    gaps = sum((jnp.where(wanted >= e, PAD - HD, 0) for e in edges), jnp.zeros_like(wanted))
    wanted = jnp.where((inner >= 0) & (inner < count), wanted + gaps, -1)
    return (row == wanted).astype(F32).astype(BF16)


def spreaders(qs, ps):
    for tile in range(TILES):
        shard = lane_shards(tile)[0]
        qs[tile] = choice(qlow(tile), QWIN, 27 * shard, 0, 27, 54, (HD, 2 * HD))
        low = plow(tile)
        ps[tile, :, 0:128] = choice(low, PWIN, 18 * shard, 0, 18, 36, ())
        ps[tile, :, 128:256] = choice(low, PWIN, 18 * shard, 18, 9, 36, ())
        ps[tile, :, 256:384] = choice(low, PWIN, 18 * shard + 9, 18, 9, 36, ())


def qkv_terms(qs, hcat, dpk, mq, g):
    for x in range(4):
        for t in range(4):
            tile = x * 4 + t
            low = qlow(tile)
            spread = dot(dpk[:, low : low + QWIN], qs[tile])
            mq[:, t * 128 : (t + 1) * 128] = spread.astype(BF16)
        total = dot(hcat[...], mq[...]).astype(BF16)
        for y_lo in range(2):
            for y_hi in range(2):
                for p in range(2):
                    row = y_lo * QROWS + p * 144
                    g[p][x, y_hi, y_lo] = total[row : row + 144, y_hi * 256 : (y_hi + 1) * 256]


def proj_terms(ps, a01, a2, dy, mp, g):
    for x in range(4):
        for t in range(4):
            tile = x * 4 + t
            low = plow(tile)
            spread = dot(dy[:, low : low + PWIN], ps[tile]).astype(BF16)
            for j in range(3):
                mp[j, :, t * 128 : (t + 1) * 128] = spread[:, j * 128 : (j + 1) * 128]
        most = dot(a01[...], mp[0])
        for p in range(2):
            last = dot(a2[...], mp[1 + p])
            for y_lo in range(2):
                row = y_lo * 96 + p * 48
                total = (most[row : row + 48] + last[y_lo * 48 : y_lo * 48 + 48]).astype(BF16)
                for y_hi in range(2):
                    g[2 + p][x, y_hi, y_lo] = total[:, y_hi * 256 : (y_hi + 1) * 256]


class Ring:
    def __init__(self, copy, block, relay, near, place, along):
        self.copy, self.block, self.relay, self.near = copy, block, relay, near
        self.up, self.down = lax.rem(place + 1, 4), lax.rem(place + 3, 4)
        self.two = lax.rem(place + 2, 4)
        self.to_up, self.to_down = along(1), along(3)

    def first(self):
        copy, block, near = self.copy, self.block, self.near
        self.on_way = (
            copy(block(self.two, 0), self.relay.at[0], self.to_up),
            copy(block(self.two, 1), self.relay.at[1], self.to_down),
        )
        self.copies = [
            copy(block(self.up, 1), near.at[0, 1], self.to_up),
            copy(block(self.down, 0), near.at[1, 0], self.to_down),
        ]

    def second(self):
        copy, block, near = self.copy, self.block, self.near
        steps = ((self.up, 0, self.to_up), (self.down, 1, self.to_down))
        for side, (place, half, to) in enumerate(steps):
            self.on_way[side].wait()
            ref = block(place, half)
            ref[...] = (ref[...].astype(F32) + self.relay[side].astype(F32)).astype(BF16)
            self.copies.append(copy(ref, near.at[side, half], to))

    def total(self, own):
        for c in self.copies:
            c.wait()
        near = self.near[0].astype(F32) + self.near[1].astype(F32)
        return own.astype(F32) + near.reshape(own.shape)


class Part:
    def __init__(self, copy, refs, rows, x_first, position, along_x, along_y):
        self.copy, self.rows, self.x_first = copy, rows, x_first
        self.g, relay, near, self.h, self.r = refs
        self.x, self.y_hi, self.y_lo = position
        y = self.y_hi * 2 + self.y_lo
        if x_first:
            self.ring = Ring(copy, self.of_x, relay, near, self.x, along_x)
            self.other, self.along = y, along_y
        else:
            self.ring = Ring(copy, self.of_y, relay, near, y, along_y)
            self.other, self.along = self.x, along_x

    def of_x(self, i, half):
        return self.g.at[i, half]

    def of_y(self, i, half):
        return self.g.at[pl.ds(2 * half, 2), lax.div(i, 2), lax.rem(i, 2)]

    def first(self):
        self.ring.first()

    def second(self):
        self.ring.second()

    def across(self):
        own = self.g[self.x] if self.x_first else self.g[:, self.y_hi, self.y_lo]
        self.h[...] = self.ring.total(own.reshape(4, self.rows, 256)).astype(BF16)
        self.copies = [
            self.copy(self.h.at[lax.rem(self.other + k, 4)], self.r.at[k], self.along(k))
            for k in range(1, 4)
        ]

    def total(self):
        acc = self.h[self.other].astype(F32)
        for k, c in enumerate(self.copies):
            c.wait()
            acc = acc + self.r[k + 1].astype(F32)
        return acc


def kernel(
    x_in, dy_in, ws_in, ps_in, wt_in, pt_in,
    dx_out, sums_out,
    x_v, dy_v, ws, ps, wt, pt,
    nxb, nxr, dxb, dxr, dab, dar, otb, otr,
    qs, ks, vs, os, qt, kt, vt, ot, da, acc0, acc1, acc2,
    ht, at, hcat, a01, a2, dpk, dyf,
    spread_q, spread_p, mq, mp,
    zs, zr,
    send, recv, all_send, all_recv, local,
    *part_refs,
):
    dp, me = lax.axis_index("dp"), lax.axis_index("seq")
    core, y_lo = lax.rem(dp, 2), lax.div(dp, 2)
    y_hi, z, x = lax.rem(me, 2), lax.rem(lax.div(me, 2), 8), lax.div(me, 16)
    y = y_hi * 2 + y_lo
    n = GROUPS
    pair = at_xyz(x, y, z, 1 - core)

    def along_x(k):
        return at_xyz(lax.rem(x + k, 4), y, z, core)

    def along_y(k):
        return at_xyz(x, lax.rem(y + k, 4), z, core)

    def along_z(k):
        return at_xyz(x, y, lax.rem(z + k, 8), core)

    counts = [0, 0]

    def here(source, target):
        c = pltpu.make_async_copy(source, target, local.at[counts[0]])
        counts[0] += 1
        c.start()
        return c

    def copy(source, target, to):
        i = counts[1]
        counts[1] += 1
        c = pltpu.make_async_remote_copy(
            src_ref=source,
            dst_ref=target,
            send_sem=send.at[i],
            recv_sem=recv.at[i],
            device_id=to,
            device_id_type=MESH,
        )
        c.start()
        return c

    get_x = here(x_in, x_v)
    get_ws = here(ws_in, ws)
    get_ps = here(ps_in, ps)
    get_dy = here(dy_in, dy_v)
    get_pt = here(pt_in, pt)
    get_wt = here(wt_in, wt)

    barrier = pltpu.get_barrier_semaphore()

    @pl.loop(1, n)
    def _(i):
        pl.semaphore_signal(barrier, inc=1, device_id=(dp, lax.rem(me + i, n)), device_id_type=MESH)

    for friend in (pair, along_y(1), along_y(3)):
        pl.semaphore_signal(barrier, inc=1, device_id=friend, device_id_type=MESH)

    def exchange_start(j, source, target):
        @pl.loop(1, n)
        def _(i):
            to = lax.rem(me + i, n)
            pltpu.make_async_remote_copy(
                src_ref=source.at[to],
                dst_ref=target.at[me],
                send_sem=all_send.at[j],
                recv_sem=all_recv.at[j],
                device_id=(dp, to),
                device_id_type=MESH,
            ).start()

        return here(source.at[me], target.at[me])

    def exchange_wait(j, source, target, own):
        own.wait()
        pltpu.make_async_remote_copy(
            src_ref=source.at[pl.ds(0, n - 1)],
            dst_ref=target.at[pl.ds(0, n - 1)],
            send_sem=all_send.at[j],
            recv_sem=all_recv.at[j],
            device_id=pair,
            device_id_type=MESH,
        ).wait()

    far = pl.ds(TOK, TOK)

    def share_hidden(b):
        copies = []
        for i in range(2):
            rows = pl.ds(pl.multiple_of((i * 2 + 1 - core) * QROWS, 32), QROWS)
            copies.append(copy(ht.at[b, rows], hcat.at[b, pl.ds(i * QROWS, QROWS), far], pair))
            rows = pl.ds(pl.multiple_of((i * 2 + core) * QROWS, 32), QROWS)
            hcat[b, i * QROWS : (i + 1) * QROWS, :TOK] = ht[b, rows, :]
        return copies

    def share_attn(b):
        copies = []
        for i in range(2):
            row = (i * 2 + 1 - core) * 144
            rows = pl.ds(pl.multiple_of(row, 16), 96)
            copies.append(copy(at.at[b, rows], a01.at[b, pl.ds(i * 96, 96), far], pair))
            rows = pl.ds(pl.multiple_of(row + 96, 16), 48)
            copies.append(copy(at.at[b, rows], a2.at[b, pl.ds(i * 48, 48), far], pair))
            row = (i * 2 + core) * 144
            rows = pl.ds(pl.multiple_of(row, 16), 96)
            a01[b, i * 96 : (i + 1) * 96, :TOK] = at[b, rows, :]
            rows = pl.ds(pl.multiple_of(row + 96, 16), 48)
            a2[b, i * 48 : (i + 1) * 48, :TOK] = at[b, rows, :]
        return copies

    def share(ref, b):
        return copy(ref.at[b, pl.ds(0, TOK)], ref.at[b, far], pair)

    def parts(b):
        found = []
        for p, (rows, x_first) in enumerate(PARTS):
            refs = [ref.at[b] for ref in part_refs[p * 5 : (p + 1) * 5]]
            found.append(Part(copy, refs, rows, x_first, (x, y_hi, y_lo), along_x, along_y))
        return found

    def wait(copies):
        for c in copies:
            c.wait()

    def last(b, found):
        total = jnp.concatenate([p.total() for p in found], axis=0).T
        zs[b] = total.reshape(8, 32, ROWS).astype(BF16)
        return [copy(zs.at[b, lax.rem(z + k, 8)], zr.at[b, k], along_z(k)) for k in range(1, 8)]

    def finish(b, copies):
        acc = zs[b, z].astype(F32)
        for k in range(1, 8):
            copies[k - 1].wait()
            acc = acc + zr[b, k].astype(F32)
        sums_out[b] = acc

    SPACE, TIME = 0, 1
    space, time = parts(SPACE), parts(TIME)
    own = pl.ds(0, TOK)
    accs = (acc0, acc1, acc2)

    get_x.wait()
    source = x_v[...].astype(F32)
    normed, _ = normalize(source)
    hidden = normed.astype(BF16)
    get_ws.wait()
    project(hidden, ws, (qs, ks, vs))
    attention(qs, ks, vs, acc0, os, None)
    get_ps.wait()
    to_blocks((source + dot(os[:, :HD], ps[...])).astype(BF16), nxb)
    get_dy.wait()
    get_pt.wait()
    dyf[TIME, :TOK, :] = dy_v[...]
    da[:, :HD] = dot(dy_v[...], pt[...], NT).astype(BF16)
    da[:, HD:] = jnp.zeros((TOK, PAD - HD), BF16)
    to_blocks(da[...], dab)
    pl.semaphore_wait(barrier, n + 2)
    own_next = exchange_start(0, nxb, nxr)
    own_da = exchange_start(1, dab, dar)
    ht[SPACE] = hidden.T
    at[SPACE] = os[...].T
    hidden_s = share_hidden(SPACE)
    proj_s = share_attn(SPACE)
    proj_t = [share(dyf, TIME)]
    spreaders(spread_q, spread_p)

    get_wt.wait()
    exchange_wait(0, nxb, nxr, own_next)
    normed, _ = normalize(from_blocks(nxr).astype(F32))
    hidden = normed.astype(BF16)
    project(hidden, wt, (qt, kt, vt))
    keep = same_position()
    attention(qt, kt, vt, acc0, ot, keep)
    to_blocks(ot[...], otb)
    own_attn = exchange_start(3, otb, otr)
    ht[TIME] = hidden.T
    hidden_t = share_hidden(TIME)
    exchange_wait(1, dab, dar, own_da)
    da[...] = from_blocks(dar)
    attention_back(qt, kt, vt, ot, da, accs, keep, {})
    pack(accs, dpk.at[TIME, own])
    hidden_t.append(share(dpk, TIME))
    middle = from_blocks(nxr).astype(F32)
    to_blocks(block_back(middle, wt, dpk.at[TIME, own]).astype(BF16), dxb)
    own_dx = exchange_start(2, dxb, dxr)

    wait(hidden_t)
    qkv_terms(spread_q, hcat.at[TIME], dpk.at[TIME], mq, [p.g for p in time])
    time[0].first()
    time[1].first()
    exchange_wait(3, otb, otr, own_attn)
    at[TIME] = from_blocks(otr).T
    proj_t += share_attn(TIME)
    wait(proj_t)
    proj_terms(spread_p, a01.at[TIME], a2.at[TIME], dyf.at[TIME], mp, [p.g for p in time])
    time[2].first()
    time[3].first()

    exchange_wait(2, dxb, dxr, own_dx)
    dy = (dy_v[...].astype(F32) + from_blocks(dxr).astype(F32)).astype(BF16)
    dyf[SPACE, :TOK, :] = dy
    proj_s.append(share(dyf, SPACE))
    da[:, :HD] = dot(dy, ps[...], NT).astype(BF16)
    da[:, HD:] = jnp.zeros((TOK, PAD - HD), BF16)

    def hook_a():
        time[0].second()
        time[1].second()

    def hook_b():
        wait(proj_s)
        proj_terms(spread_p, a01.at[SPACE], a2.at[SPACE], dyf.at[SPACE], mp, [p.g for p in space])
        space[2].first()
        space[3].first()

    def hook_c():
        time[2].second()
        time[3].second()

    hooks = {0: hook_a, 3: hook_b, 6: hook_c}
    attention_back(qs, ks, vs, os, da, accs, None, hooks)
    pack(accs, dpk.at[SPACE, own])
    hidden_s.append(share(dpk, SPACE))
    for p in time:
        p.across()
    wait(hidden_s)
    qkv_terms(spread_q, hcat.at[SPACE], dpk.at[SPACE], mq, [p.g for p in space])
    space[0].first()
    space[1].first()
    space[2].second()
    space[3].second()
    along = last(TIME, time)
    dx_s = block_back(x_v[...].astype(F32), ws, dpk.at[SPACE, own])
    dx_out[...] = (dyf[SPACE, :TOK, :].astype(F32) + dx_s).astype(BF16)
    space[0].second()
    space[1].second()
    space[2].across()
    space[3].across()
    finish(TIME, along)
    space[0].across()
    space[1].across()
    finish(SPACE, last(SPACE, space))


def outputs_kernel(dx, sums, dx_out, gqs, gps, gqt, gpt):
    dx_out[...] = dx[...]
    for b, (qkv, proj) in enumerate(((gqs, gps), (gqt, gpt))):
        block = sums[b]
        qkv[...] = block[:27, :QROWS]
        proj[:, 0:96] = block[:18, QROWS:]
        proj[0:9, 96:144] = block[18:27, QROWS : QROWS + 48]
        proj[9:18, 96:144] = block[18:27, QROWS + 48 :]


def per_device(latents, out_grad, qkv_spatial, proj_spatial, qkv_temporal, proj_temporal):
    ins = [latents[0, 0], out_grad[0, 0], qkv_spatial, proj_spatial.T, qkv_temporal, proj_temporal.T]
    wide, narrow = VMEM((TOK, D), BF16), VMEM((TOK, PAD), BF16)
    qkv, proj = VMEM((3 * HD, D), BF16), VMEM((HD, D), BF16)
    blocks = VMEM((GROUPS, D // 128, OWN, 128), BF16)
    small = VMEM((GROUPS, PAD // 128, OWN, 128), BF16)
    acc = VMEM((TOK, PAD), F32)
    dma = pltpu.SemaphoreType.DMA
    part_refs = []
    for rows, _ in PARTS:
        part_refs += [
            VMEM((2, 4, 2, 2, rows, 256), BF16),
            VMEM((2, 2, 2, rows, 256), BF16),
            VMEM((2, 2, 2, 2, rows, 256), BF16),
            VMEM((2, 4, rows, 256), BF16),
            VMEM((2, 4, rows, 256), BF16),
        ]
    dx, sums = pl.pallas_call(
        kernel,
        out_shape=[
            jax.ShapeDtypeStruct((TOK, D), BF16),
            jax.ShapeDtypeStruct((2, 32, ROWS), F32),
        ],
        in_specs=[pl.BlockSpec(memory_space=pl.ANY)] * len(ins),
        out_specs=[pl.BlockSpec(memory_space=VMEM)] * 2,
        scratch_shapes=[
            wide, wide, qkv, proj, qkv, proj,
            *[blocks] * 4, *[small] * 4,
            *[narrow] * 9, acc, acc, acc,
            VMEM((2, D, TOK), BF16),
            VMEM((2, PAD, TOK), BF16),
            VMEM((2, 2 * QROWS, 2 * TOK), BF16),
            VMEM((2, 192, 2 * TOK), BF16),
            VMEM((2, 96, 2 * TOK), BF16),
            VMEM((2, 2 * TOK, 3 * PAD), BF16),
            VMEM((2, 2 * TOK, D), BF16),
            VMEM((TILES, QWIN, 128), BF16),
            VMEM((TILES, PWIN, 384), BF16),
            VMEM((2 * TOK, 512), BF16),
            VMEM((3, 2 * TOK, 512), BF16),
            *[VMEM((2, 8, 32, ROWS), BF16)] * 2,
            dma((102,)), dma((102,)), dma((4,)), dma((4,)), dma((10,)),
            *part_refs,
        ],
        name="both_blocks",
        compiler_params=pltpu.CompilerParams(
            collective_id=0, has_side_effects=True, vmem_limit_bytes=LIMIT
        ),
    )(*ins)
    vmem = pl.BlockSpec(memory_space=VMEM)
    f32 = [jax.ShapeDtypeStruct(s, F32) for s in ((27, 288), (18, 144), (27, 288), (18, 144))]
    dx, qkv_s, proj_s, qkv_t, proj_t = pl.pallas_call(
        outputs_kernel,
        out_shape=[jax.ShapeDtypeStruct((TOK, D), BF16), *f32],
        in_specs=[vmem] * 2,
        out_specs=[vmem] * 5,
        name="outputs",
    )(dx, sums)
    return dx[None, None], qkv_s, proj_s, qkv_t, proj_t


def solution(mesh):
    placed = (P("dp", "seq", None, None), P("dp", "seq", None, None), P(), P(), P(), P())
    return jax.shard_map(
        per_device,
        mesh=mesh,
        in_specs=placed,
        out_specs=(
            P("dp", "seq", None, None),
            P("seq", "dp"),
            P("seq", "dp"),
            P("seq", "dp"),
            P("seq", "dp"),
        ),
        check_vma=False,
    )
```

```python
import jax
import jax.numpy as jnp
from jax import lax
from jax.experimental import pallas as pl
from jax.experimental.pallas import tpu as pltpu
from jax.sharding import PartitionSpec as P

HDIM = 72
HEADS = 8
HD = HDIM * HEADS
PAD = 640
D = 1152
TOK = 256
GROUPS = 64
OWN = TOK // GROUPS
EPS = 1e-06
SCALE = HDIM ** (-0.5)
NEG = -1e30
MESH = pl.DeviceIdType.MESH
VMEM = pltpu.VMEM
F32 = jnp.float32
BF16 = jnp.bfloat16
LIMIT = 60 * 2**20

QROWS = 288
PROWS = 96
ROWS = QROWS + PROWS
PARTS = ((80, True), (80, False), (64, True), (64, False), (48, True), (48, False))
WAVES = ((0, 160), (160, 128))
TILES = 16
QWIN = 384
PWIN = 256
WIDE = 1792


def dot(a, b, dims=((1,), (0,))):
    return lax.dot_general(a, b, (dims, ((), ())), preferred_element_type=F32)


NT = ((1,), (1,))
TN = ((0,), (0,))


def window(head):
    low = head * HDIM // 128 * 128
    return low, -(-(head + 1) * HDIM // 128) * 128


def head_mask(head, low, high):
    lane = lax.broadcasted_iota(jnp.int32, (1, high - low), 1) + low
    return ((lane >= head * HDIM) & (lane < (head + 1) * HDIM)).astype(F32).astype(BF16)


def normalize(x):
    inverse = lax.rsqrt(jnp.mean(x * x, axis=-1, keepdims=True) + EPS)
    return x * inverse, inverse


def project(hidden, w_ref, targets):
    for i, target in enumerate(targets):
        target[:, :HD] = dot(hidden, w_ref[i * HD : (i + 1) * HD, :], NT).astype(BF16)
        target[:, HD:] = jnp.zeros((TOK, PAD - HD), BF16)


def softmax(qm, k, keep):
    s = dot(qm, k, NT) * SCALE
    if keep is not None:
        s = jnp.where(keep, s, NEG)
    e = jnp.exp(s - jnp.max(s, axis=-1, keepdims=True))
    return e * (1.0 / jnp.sum(e, axis=-1, keepdims=True))


def same_position():
    rows = lax.broadcasted_iota(jnp.int32, (TOK, TOK), 0)
    columns = lax.broadcasted_iota(jnp.int32, (TOK, TOK), 1)
    return lax.rem(rows, OWN) == lax.rem(columns, OWN)


def attention(q, k, v, acc, attn, kept, keep):
    acc[...] = jnp.zeros_like(acc)
    for h in range(HEADS):
        low, high = window(h)
        mask = head_mask(h, low, high)
        probs = softmax(q[:, low:high] * mask, k[:, low:high], keep)
        kept[h] = probs.astype(BF16)
        acc[:, low:high] += dot(kept[h], v[:, low:high] * mask)
    attn[...] = acc[...].astype(BF16)


def attention_back(q, k, v, attn, da, accs, kept, hooks):
    for acc in accs:
        acc[...] = jnp.zeros_like(acc)
    dq, dk, dv = accs
    for h in range(HEADS):
        if h in hooks:
            hooks[h]()
        low, high = window(h)
        mask = head_mask(h, low, high)
        qm = q[:, low:high] * mask
        km = k[:, low:high] * mask
        dam = da[:, low:high] * mask
        d_probs = dot(dam, v[:, low:high], NT)
        dv[:, low:high] += dot(kept[h], dam, TN)
        offset = jnp.sum(dam.astype(F32) * attn[:, low:high].astype(F32), axis=-1, keepdims=True)
        ds = (kept[h].astype(F32) * ((d_probs - offset) * SCALE)).astype(BF16)
        dq[:, low:high] += dot(ds, km)
        dk[:, low:high] += dot(ds, qm, TN)


def pack(accs, dpk):
    for i, acc in enumerate(accs):
        dpk[:, i * HD : (i + 1) * HD] = acc[:, :HD].astype(BF16)
    dpk[:, 3 * HD :] = jnp.zeros((TOK, WIDE - 3 * HD), BF16)


def block_back(x, w_ref, dpk):
    d_hidden = dot(dpk[:, : 3 * HD], w_ref[...])
    normed, inverse = normalize(x)
    along = jnp.mean(d_hidden * normed, axis=-1, keepdims=True)
    return inverse * (d_hidden - normed * along)


def to_blocks(value, ref):
    for t in range(ref.shape[1]):
        ref[:, t, :, :] = value[:, t * 128 : (t + 1) * 128].reshape(GROUPS, OWN, 128)


def from_blocks(ref):
    return jnp.concatenate([ref[:, t, :, :].reshape(TOK, 128) for t in range(ref.shape[1])], axis=1)


def at_xyz(x, y, z, core):
    return lax.rem(y, 2) * 2 + core, (x * 8 + z) * 2 + lax.div(y, 2)


def lane_shards(tile):
    x, y_hi, z_hi = tile // 4, tile // 2 % 2, tile % 2
    return [(x * 8 + z_hi * 4 + i) * 2 + y_hi for i in range(4)]


def qlow(tile):
    return min(27 * lane_shards(tile)[0] // 128 * 128, WIDE - QWIN)


def plow(tile):
    return min(18 * lane_shards(tile)[0] // 128 * 128, D - PWIN)


def choice(low, window, lead, first, count, step):
    row = lax.broadcasted_iota(jnp.int32, (window, 128), 0) + low
    lane = lax.broadcasted_iota(jnp.int32, (1, 128), 1)
    inner = (lane & 31) - first
    wanted = lead + lax.shift_right_logical(lane, 5) * step + inner
    wanted = jnp.where((inner >= 0) & (inner < count), wanted, -1)
    return (row == wanted).astype(F32).astype(BF16)


def spreaders(qs, ps):
    for tile in range(TILES):
        shard = lane_shards(tile)[0]
        qs[tile] = choice(qlow(tile), QWIN, 27 * shard, 0, 27, 54)
        low = plow(tile)
        ps[tile, :, 0:128] = choice(low, PWIN, 18 * shard, 0, 18, 36)
        ps[tile, :, 128:256] = choice(low, PWIN, 18 * shard, 18, 9, 36)
        ps[tile, :, 256:384] = choice(low, PWIN, 18 * shard + 9, 18, 9, 36)


def qkv_spread(qs, dpk, mq):
    for tile in range(TILES):
        low = qlow(tile)
        spread = dot(dpk[:, low : low + QWIN], qs[tile])
        mq[:, tile * 128 : (tile + 1) * 128] = spread.astype(BF16)


def qkv_terms(wave, hcat, mq, g):
    first, rows = WAVES[wave]
    for x in range(4):
        total = dot(hcat[2 * first : 2 * (first + rows)], mq[:, x * 512 : (x + 1) * 512])
        total = total.astype(BF16)
        for y_lo in range(2):
            for y_hi in range(2):
                for p in range(2):
                    row = y_lo * rows + p * (rows // 2)
                    block = total[row : row + rows // 2, y_hi * 256 : (y_hi + 1) * 256]
                    g[2 * wave + p][x, y_hi, y_lo] = block


def proj_terms(ps, a01, a2, dy, mp, g):
    for x in range(4):
        for t in range(4):
            tile = x * 4 + t
            low = plow(tile)
            spread = dot(dy[:, low : low + PWIN], ps[tile]).astype(BF16)
            for j in range(3):
                mp[j, :, t * 128 : (t + 1) * 128] = spread[:, j * 128 : (j + 1) * 128]
        most = dot(a01[...], mp[0])
        for p in range(2):
            last = dot(a2[...], mp[1 + p])
            for y_lo in range(2):
                row = y_lo * 96 + p * 48
                total = (most[row : row + 48] + last[y_lo * 48 : y_lo * 48 + 48]).astype(BF16)
                for y_hi in range(2):
                    g[4 + p][x, y_hi, y_lo] = total[:, y_hi * 256 : (y_hi + 1) * 256]


class Ring:
    def __init__(self, copy, block, relay, near, place, along):
        self.copy, self.block, self.relay, self.near = copy, block, relay, near
        self.up, self.down = lax.rem(place + 1, 4), lax.rem(place + 3, 4)
        self.two = lax.rem(place + 2, 4)
        self.to_up, self.to_down = along(1), along(3)

    def first(self):
        copy, block, near = self.copy, self.block, self.near
        self.on_way = (
            copy(block(self.two, 0), self.relay.at[0], self.to_up),
            copy(block(self.two, 1), self.relay.at[1], self.to_down),
        )
        self.copies = [
            copy(block(self.up, 1), near.at[0, 1], self.to_up),
            copy(block(self.down, 0), near.at[1, 0], self.to_down),
        ]

    def second(self):
        copy, block, near = self.copy, self.block, self.near
        steps = ((self.up, 0, self.to_up), (self.down, 1, self.to_down))
        for side, (place, half, to) in enumerate(steps):
            self.on_way[side].wait()
            ref = block(place, half)
            ref[...] = (ref[...].astype(F32) + self.relay[side].astype(F32)).astype(BF16)
            self.copies.append(copy(ref, near.at[side, half], to))

    def total(self, own):
        for c in self.copies:
            c.wait()
        near = self.near[0].astype(F32) + self.near[1].astype(F32)
        return own.astype(F32) + near.reshape(own.shape)


class Part:
    def __init__(self, copy, refs, rows, x_first, position, along_x, along_y):
        self.copy, self.rows, self.x_first = copy, rows, x_first
        self.g, relay, near, self.h, self.r = refs
        self.x, self.y_hi, self.y_lo = position
        y = self.y_hi * 2 + self.y_lo
        if x_first:
            self.ring = Ring(copy, self.of_x, relay, near, self.x, along_x)
            self.other, self.along = y, along_y
        else:
            self.ring = Ring(copy, self.of_y, relay, near, y, along_y)
            self.other, self.along = self.x, along_x

    def of_x(self, i, half):
        return self.g.at[i, half]

    def of_y(self, i, half):
        return self.g.at[pl.ds(2 * half, 2), lax.div(i, 2), lax.rem(i, 2)]

    def first(self):
        self.ring.first()

    def second(self):
        self.ring.second()

    def across(self):
        own = self.g[self.x] if self.x_first else self.g[:, self.y_hi, self.y_lo]
        self.h[...] = self.ring.total(own.reshape(4, self.rows, 256)).astype(BF16)
        self.copies = [
            self.copy(self.h.at[lax.rem(self.other + k, 4)], self.r.at[k], self.along(k))
            for k in range(1, 4)
        ]

    def total(self):
        acc = self.h[self.other].astype(F32)
        for k, c in enumerate(self.copies):
            c.wait()
            acc = acc + self.r[k + 1].astype(F32)
        return acc


def kernel(
    x_in, dy_in, ws_in, ps_in, wt_in, pt_in,
    dx_out, sums_out,
    x_v, dy_v, ws, ps, wt, pt,
    nxb, nxr, dxb, dxr, dab, dar, otb, otr,
    qs, ks, vs, os, qt, kt, vt, ot, da, acc0, acc1, acc2, kept_s, kept_t,
    ht, at, hcat, a01, a2, dpk, dyf,
    spread_q, spread_p, mq, mp,
    zs1, zr1, zs2, zr2,
    send, recv, all_send, all_recv, local,
    *part_refs,
):
    dp, me = lax.axis_index("dp"), lax.axis_index("seq")
    core, y_lo = lax.rem(dp, 2), lax.div(dp, 2)
    y_hi, z, x = lax.rem(me, 2), lax.rem(lax.div(me, 2), 8), lax.div(me, 16)
    y = y_hi * 2 + y_lo
    n = GROUPS
    pair = at_xyz(x, y, z, 1 - core)

    def along_x(k):
        return at_xyz(lax.rem(x + k, 4), y, z, core)

    def along_y(k):
        return at_xyz(x, lax.rem(y + k, 4), z, core)

    def along_z(k):
        return at_xyz(x, y, lax.rem(z + k, 8), core)

    counts = [0, 0]

    def here(source, target):
        c = pltpu.make_async_copy(source, target, local.at[counts[0]])
        counts[0] += 1
        c.start()
        return c

    def copy(source, target, to):
        i = counts[1]
        counts[1] += 1
        c = pltpu.make_async_remote_copy(
            src_ref=source,
            dst_ref=target,
            send_sem=send.at[i],
            recv_sem=recv.at[i],
            device_id=to,
            device_id_type=MESH,
        )
        c.start()
        return c

    get_x = here(x_in, x_v)
    get_ws = here(ws_in, ws)
    get_ps = here(ps_in, ps)
    get_dy = here(dy_in, dy_v)
    get_pt = here(pt_in, pt)
    get_wt = here(wt_in, wt)

    barrier = pltpu.get_barrier_semaphore()

    @pl.loop(1, n)
    def _(i):
        pl.semaphore_signal(barrier, inc=1, device_id=(dp, lax.rem(me + i, n)), device_id_type=MESH)

    for friend in (pair, along_y(1), along_y(3)):
        pl.semaphore_signal(barrier, inc=1, device_id=friend, device_id_type=MESH)

    def exchange_start(j, source, target):
        @pl.loop(1, n)
        def _(i):
            to = lax.rem(me + i, n)
            pltpu.make_async_remote_copy(
                src_ref=source.at[to],
                dst_ref=target.at[me],
                send_sem=all_send.at[j],
                recv_sem=all_recv.at[j],
                device_id=(dp, to),
                device_id_type=MESH,
            ).start()

        return here(source.at[me], target.at[me])

    def exchange_wait(j, source, target, own):
        own.wait()
        pltpu.make_async_remote_copy(
            src_ref=source.at[pl.ds(0, n - 1)],
            dst_ref=target.at[pl.ds(0, n - 1)],
            send_sem=all_send.at[j],
            recv_sem=all_recv.at[j],
            device_id=pair,
            device_id_type=MESH,
        ).wait()

    far = pl.ds(TOK, TOK)

    def share_hidden(b):
        copies = []
        for i in range(2):
            for first, rows in WAVES:
                to = pl.ds(2 * first + i * rows, rows)
                row = pl.multiple_of((i * 2 + 1 - core) * QROWS + first, 32)
                copies.append(copy(ht.at[b, pl.ds(row, rows)], hcat.at[b, to, far], pair))
                row = pl.multiple_of((i * 2 + core) * QROWS + first, 32)
                hcat[b, to, :TOK] = ht[b, pl.ds(row, rows), :]
        return copies

    def share_attn(b):
        copies = []
        for i in range(2):
            row = (i * 2 + 1 - core) * 144
            rows = pl.ds(pl.multiple_of(row, 16), 96)
            copies.append(copy(at.at[b, rows], a01.at[b, pl.ds(i * 96, 96), far], pair))
            rows = pl.ds(pl.multiple_of(row + 96, 16), 48)
            copies.append(copy(at.at[b, rows], a2.at[b, pl.ds(i * 48, 48), far], pair))
            row = (i * 2 + core) * 144
            rows = pl.ds(pl.multiple_of(row, 16), 96)
            a01[b, i * 96 : (i + 1) * 96, :TOK] = at[b, rows, :]
            rows = pl.ds(pl.multiple_of(row + 96, 16), 48)
            a2[b, i * 48 : (i + 1) * 48, :TOK] = at[b, rows, :]
        return copies

    def share(ref, b):
        return copy(ref.at[b, pl.ds(0, TOK)], ref.at[b, far], pair)

    def parts(b):
        found = []
        for p, (rows, x_first) in enumerate(PARTS):
            refs = [ref.at[b] for ref in part_refs[p * 5 : (p + 1) * 5]]
            found.append(Part(copy, refs, rows, x_first, (x, y_hi, y_lo), along_x, along_y))
        return found

    def wait(copies):
        for c in copies:
            c.wait()

    def last(b, found, zs, zr):
        total = jnp.concatenate([p.total() for p in found], axis=0).T
        zs[b] = total.reshape(zs.shape[1:]).astype(BF16)
        return [copy(zs.at[b, lax.rem(z + k, 8)], zr.at[b, k], along_z(k)) for k in range(1, 8)]

    def last_first(b, found):
        return last(b, [found[0], found[1], found[4], found[5]], zs1, zr1)

    def last_second(b, found):
        return last(b, [found[2], found[3]], zs2, zr2)

    def finish(b, copies, zs, zr, lanes):
        acc = zs[b, z].astype(F32)
        for k in range(1, 8):
            copies[k - 1].wait()
            acc = acc + zr[b, k].astype(F32)
        sums_out[b, :, lanes] = acc

    def finish_both(b, first, second):
        finish(b, first, zs1, zr1, slice(0, 256))
        finish(b, second, zs2, zr2, slice(256, 384))

    SPACE, TIME = 0, 1
    space, time = parts(SPACE), parts(TIME)
    own = pl.ds(0, TOK)
    accs = (acc0, acc1, acc2)

    get_x.wait()
    source = x_v[...].astype(F32)
    normed, _ = normalize(source)
    hidden = normed.astype(BF16)
    get_ws.wait()
    project(hidden, ws, (qs, ks, vs))
    attention(qs, ks, vs, acc0, os, kept_s, None)
    get_ps.wait()
    to_blocks((source + dot(os[:, :HD], ps[...])).astype(BF16), nxb)
    pl.semaphore_wait(barrier, n + 2)
    own_next = exchange_start(0, nxb, nxr)
    get_dy.wait()
    get_pt.wait()
    da[:, :HD] = dot(dy_v[...], pt[...], NT).astype(BF16)
    da[:, HD:] = jnp.zeros((TOK, PAD - HD), BF16)
    to_blocks(da[...], dab)
    own_da = exchange_start(1, dab, dar)
    dyf[TIME, :TOK, :] = dy_v[...]
    ht[SPACE] = hidden.T
    at[SPACE] = os[...].T
    hidden_s = share_hidden(SPACE)
    proj_s = share_attn(SPACE)
    proj_t = [share(dyf, TIME)]
    spreaders(spread_q, spread_p)

    get_wt.wait()
    exchange_wait(0, nxb, nxr, own_next)
    normed, _ = normalize(from_blocks(nxr).astype(F32))
    hidden = normed.astype(BF16)
    project(hidden, wt, (qt, kt, vt))
    keep = same_position()
    attention(qt, kt, vt, acc0, ot, kept_t, keep)
    to_blocks(ot[...], otb)
    own_attn = exchange_start(3, otb, otr)
    ht[TIME] = hidden.T
    hidden_t = share_hidden(TIME)
    exchange_wait(1, dab, dar, own_da)
    da[...] = from_blocks(dar)
    attention_back(qt, kt, vt, ot, da, accs, kept_t, {})
    pack(accs, dpk.at[TIME, own])
    hidden_t.append(share(dpk, TIME))
    middle = from_blocks(nxr).astype(F32)
    to_blocks(block_back(middle, wt, dpk.at[TIME, own]).astype(BF16), dxb)
    own_dx = exchange_start(2, dxb, dxr)

    def both(found, p, step):
        getattr(found[2 * p], step)()
        getattr(found[2 * p + 1], step)()

    wait(hidden_t)
    qkv_spread(spread_q, dpk.at[TIME], mq)
    for wave in range(2):
        qkv_terms(wave, hcat.at[TIME], mq, [p.g for p in time])
        both(time, wave, "first")
    exchange_wait(3, otb, otr, own_attn)
    at[TIME] = from_blocks(otr).T
    proj_t += share_attn(TIME)
    wait(proj_t)
    proj_terms(spread_p, a01.at[TIME], a2.at[TIME], dyf.at[TIME], mp, [p.g for p in time])
    both(time, 2, "first")

    exchange_wait(2, dxb, dxr, own_dx)
    dy = (dy_v[...].astype(F32) + from_blocks(dxr).astype(F32)).astype(BF16)
    dyf[SPACE, :TOK, :] = dy
    proj_s.append(share(dyf, SPACE))
    da[:, :HD] = dot(dy, ps[...], NT).astype(BF16)
    da[:, HD:] = jnp.zeros((TOK, PAD - HD), BF16)

    def seconds_qkv():
        both(time, 0, "second")
        both(time, 1, "second")

    def proj_set_out():
        wait(proj_s)
        proj_terms(spread_p, a01.at[SPACE], a2.at[SPACE], dyf.at[SPACE], mp, [p.g for p in space])
        both(space, 2, "first")

    def seconds_proj():
        both(time, 2, "second")

    hooks = {0: seconds_qkv, 5: seconds_proj}
    attention_back(qs, ks, vs, os, da, accs, kept_s, hooks)
    pack(accs, dpk.at[SPACE, own])
    hidden_s.append(share(dpk, SPACE))
    proj_set_out()
    for p in time:
        p.across()
    wait(hidden_s)
    qkv_spread(spread_q, dpk.at[SPACE], mq)
    for wave in range(2):
        qkv_terms(wave, hcat.at[SPACE], mq, [p.g for p in space])
        both(space, wave, "first")
    both(space, 2, "second")
    along_t = last_first(TIME, time), last_second(TIME, time)
    both(space, 0, "second")
    both(space, 1, "second")
    both(space, 2, "across")
    dx_s = block_back(x_v[...].astype(F32), ws, dpk.at[SPACE, own])
    dx_out[...] = (dyf[SPACE, :TOK, :].astype(F32) + dx_s).astype(BF16)
    both(space, 0, "across")
    both(space, 1, "across")
    finish_both(TIME, *along_t)
    along_1 = last_first(SPACE, space)
    finish_both(SPACE, along_1, last_second(SPACE, space))


def outputs_kernel(dx, sums, dx_out, gqs, gps, gqt, gpt):
    dx_out[...] = dx[...]
    for b, (qkv, proj) in enumerate(((gqs, gps), (gqt, gpt))):
        block = sums[b]
        qkv[:, 0:160] = block[:27, 0:160]
        qkv[:, 160:QROWS] = block[:27, 256:ROWS]
        proj[:, 0:96] = block[:18, 160:256]
        proj[0:9, 96:144] = block[18:27, 160:208]
        proj[9:18, 96:144] = block[18:27, 208:256]


def per_device(latents, out_grad, qkv_spatial, proj_spatial, qkv_temporal, proj_temporal):
    ins = [latents[0, 0], out_grad[0, 0], qkv_spatial, proj_spatial.T, qkv_temporal, proj_temporal.T]
    wide, narrow = VMEM((TOK, D), BF16), VMEM((TOK, PAD), BF16)
    qkv, proj = VMEM((3 * HD, D), BF16), VMEM((HD, D), BF16)
    blocks = VMEM((GROUPS, D // 128, OWN, 128), BF16)
    small = VMEM((GROUPS, PAD // 128, OWN, 128), BF16)
    acc = VMEM((TOK, PAD), F32)
    dma = pltpu.SemaphoreType.DMA
    part_refs = []
    for rows, _ in PARTS:
        part_refs += [
            VMEM((2, 4, 2, 2, rows, 256), BF16),
            VMEM((2, 2, 2, rows, 256), BF16),
            VMEM((2, 2, 2, 2, rows, 256), BF16),
            VMEM((2, 4, rows, 256), BF16),
            VMEM((2, 4, rows, 256), BF16),
        ]
    dx, sums = pl.pallas_call(
        kernel,
        out_shape=[
            jax.ShapeDtypeStruct((TOK, D), BF16),
            jax.ShapeDtypeStruct((2, 32, ROWS), F32),
        ],
        in_specs=[pl.BlockSpec(memory_space=pl.ANY)] * len(ins),
        out_specs=[pl.BlockSpec(memory_space=VMEM)] * 2,
        scratch_shapes=[
            wide, wide, qkv, proj, qkv, proj,
            *[blocks] * 4, *[small] * 4,
            *[narrow] * 9, acc, acc, acc,
            *[VMEM((HEADS, TOK, TOK), BF16)] * 2,
            VMEM((2, D, TOK), BF16),
            VMEM((2, PAD, TOK), BF16),
            VMEM((2, 2 * QROWS, 2 * TOK), BF16),
            VMEM((2, 192, 2 * TOK), BF16),
            VMEM((2, 96, 2 * TOK), BF16),
            VMEM((2, 2 * TOK, WIDE), BF16),
            VMEM((2, 2 * TOK, D), BF16),
            VMEM((TILES, QWIN, 128), BF16),
            VMEM((TILES, PWIN, 384), BF16),
            VMEM((2 * TOK, TILES * 128), BF16),
            VMEM((3, 2 * TOK, 512), BF16),
            *[VMEM((2, 8, 32, 256), BF16)] * 2,
            *[VMEM((2, 8, 32, 128), BF16)] * 2,
            dma((156,)), dma((156,)), dma((4,)), dma((4,)), dma((10,)),
            *part_refs,
        ],
        name="both_blocks",
        compiler_params=pltpu.CompilerParams(
            collective_id=0, has_side_effects=True, vmem_limit_bytes=LIMIT
        ),
    )(*ins)
    vmem = pl.BlockSpec(memory_space=VMEM)
    f32 = [jax.ShapeDtypeStruct(s, F32) for s in ((27, 288), (18, 144), (27, 288), (18, 144))]
    dx, qkv_s, proj_s, qkv_t, proj_t = pl.pallas_call(
        outputs_kernel,
        out_shape=[jax.ShapeDtypeStruct((TOK, D), BF16), *f32],
        in_specs=[vmem] * 2,
        out_specs=[vmem] * 5,
        name="outputs",
    )(dx, sums)
    return dx[None, None], qkv_s, proj_s, qkv_t, proj_t


def solution(mesh):
    placed = (P("dp", "seq", None, None), P("dp", "seq", None, None), P(), P(), P(), P())
    return jax.shard_map(
        per_device,
        mesh=mesh,
        in_specs=placed,
        out_specs=(
            P("dp", "seq", None, None),
            P("seq", "dp"),
            P("seq", "dp"),
            P("seq", "dp"),
            P("seq", "dp"),
        ),
        check_vma=False,
    )
```

```python
import jax
import jax.numpy as jnp
from jax import lax
from jax.experimental import pallas as pl
from jax.experimental.pallas import tpu as pltpu
from jax.sharding import PartitionSpec as P

HDIM = 72
HEADS = 8
HD = HDIM * HEADS
PAD = 640
D = 1152
TOK = 256
GROUPS = 64
OWN = TOK // GROUPS
EPS = 1e-06
SCALE = HDIM ** (-0.5)
NEG = -1e30
MESH = pl.DeviceIdType.MESH
VMEM = pltpu.VMEM
F32 = jnp.float32
BF16 = jnp.bfloat16
LIMIT = 60 * 2**20

QROWS = 288
PROWS = 96
ROWS = QROWS + PROWS
PARTS = ((64, True), (64, False), (80, True), (80, False), (48, True), (48, False))
WAVES = ((0, 128), (128, 160))
TILES = 16
QWIN = 384
PWIN = 256
WIDE = 1792


def dot(a, b, dims=((1,), (0,))):
    return lax.dot_general(a, b, (dims, ((), ())), preferred_element_type=F32)


NT = ((1,), (1,))
TN = ((0,), (0,))


def window(head):
    low = head * HDIM // 128 * 128
    return low, -(-(head + 1) * HDIM // 128) * 128


def head_mask(head, low, high):
    lane = lax.broadcasted_iota(jnp.int32, (1, high - low), 1) + low
    return ((lane >= head * HDIM) & (lane < (head + 1) * HDIM)).astype(F32).astype(BF16)


def normalize(x):
    inverse = lax.rsqrt(jnp.mean(x * x, axis=-1, keepdims=True) + EPS)
    return x * inverse, inverse


def project(hidden, w_ref, targets):
    for i, target in enumerate(targets):
        target[:, :HD] = dot(hidden, w_ref[i * HD : (i + 1) * HD, :], NT).astype(BF16)
        target[:, HD:] = jnp.zeros((TOK, PAD - HD), BF16)


def softmax(qm, k, keep):
    s = dot(qm, k, NT) * SCALE
    if keep is not None:
        s = jnp.where(keep, s, NEG)
    e = jnp.exp(s - jnp.max(s, axis=-1, keepdims=True))
    return e * (1.0 / jnp.sum(e, axis=-1, keepdims=True))


def same_position():
    rows = lax.broadcasted_iota(jnp.int32, (TOK, TOK), 0)
    columns = lax.broadcasted_iota(jnp.int32, (TOK, TOK), 1)
    return lax.rem(rows, OWN) == lax.rem(columns, OWN)


def attention(q, k, v, acc, attn, kept, keep):
    acc[...] = jnp.zeros_like(acc)
    for h in range(HEADS):
        low, high = window(h)
        mask = head_mask(h, low, high)
        probs = softmax(q[:, low:high] * mask, k[:, low:high], keep)
        kept[h] = probs.astype(BF16)
        acc[:, low:high] += dot(kept[h], v[:, low:high] * mask)
    attn[...] = acc[...].astype(BF16)


def attention_back(q, k, v, attn, da, accs, kept, hooks):
    for acc in accs:
        acc[...] = jnp.zeros_like(acc)
    dq, dk, dv = accs
    for h in range(HEADS):
        if h in hooks:
            hooks[h]()
        low, high = window(h)
        mask = head_mask(h, low, high)
        qm = q[:, low:high] * mask
        km = k[:, low:high] * mask
        dam = da[:, low:high] * mask
        d_probs = dot(dam, v[:, low:high], NT)
        dv[:, low:high] += dot(kept[h], dam, TN)
        offset = jnp.sum(dam.astype(F32) * attn[:, low:high].astype(F32), axis=-1, keepdims=True)
        ds = (kept[h].astype(F32) * ((d_probs - offset) * SCALE)).astype(BF16)
        dq[:, low:high] += dot(ds, km)
        dk[:, low:high] += dot(ds, qm, TN)


def pack(accs, dpk):
    for i, acc in enumerate(accs):
        dpk[:, i * HD : (i + 1) * HD] = acc[:, :HD].astype(BF16)
    dpk[:, 3 * HD :] = jnp.zeros((TOK, WIDE - 3 * HD), BF16)


def block_back(x, w_ref, dpk):
    d_hidden = dot(dpk[:, : 3 * HD], w_ref[...])
    normed, inverse = normalize(x)
    along = jnp.mean(d_hidden * normed, axis=-1, keepdims=True)
    return inverse * (d_hidden - normed * along)


def to_blocks(value, ref):
    for t in range(ref.shape[1]):
        ref[:, t, :, :] = value[:, t * 128 : (t + 1) * 128].reshape(GROUPS, OWN, 128)


def from_blocks(ref):
    return jnp.concatenate([ref[:, t, :, :].reshape(TOK, 128) for t in range(ref.shape[1])], axis=1)


def at_xyz(x, y, z, core):
    return lax.rem(y, 2) * 2 + core, (x * 8 + z) * 2 + lax.div(y, 2)


def lane_shards(tile):
    x, y_hi, z_hi = tile // 4, tile // 2 % 2, tile % 2
    return [(x * 8 + z_hi * 4 + i) * 2 + y_hi for i in range(4)]


def qlow(tile):
    return min(27 * lane_shards(tile)[0] // 128 * 128, WIDE - QWIN)


def plow(tile):
    return min(18 * lane_shards(tile)[0] // 128 * 128, D - PWIN)


def choice(low, window, lead, first, count, step):
    row = lax.broadcasted_iota(jnp.int32, (window, 128), 0) + low
    lane = lax.broadcasted_iota(jnp.int32, (1, 128), 1)
    inner = (lane & 31) - first
    wanted = lead + lax.shift_right_logical(lane, 5) * step + inner
    wanted = jnp.where((inner >= 0) & (inner < count), wanted, -1)
    return (row == wanted).astype(F32).astype(BF16)


def spreaders(qs, ps):
    for tile in range(TILES):
        shard = lane_shards(tile)[0]
        qs[tile] = choice(qlow(tile), QWIN, 27 * shard, 0, 27, 54)
        low = plow(tile)
        ps[tile, :, 0:128] = choice(low, PWIN, 18 * shard, 0, 18, 36)
        ps[tile, :, 128:256] = choice(low, PWIN, 18 * shard, 18, 9, 36)
        ps[tile, :, 256:384] = choice(low, PWIN, 18 * shard + 9, 18, 9, 36)


def qkv_spread(qs, dpk, mq, rows):
    for tile in range(TILES):
        low = qlow(tile)
        spread = dot(dpk[rows, low : low + QWIN], qs[tile])
        mq[rows, tile * 128 : (tile + 1) * 128] = spread.astype(BF16)


def qkv_terms(wave, hcat, mq, g):
    first, rows = WAVES[wave]
    for x in range(4):
        total = dot(hcat[2 * first : 2 * (first + rows)], mq[:, x * 512 : (x + 1) * 512])
        total = total.astype(BF16)
        for y_lo in range(2):
            for y_hi in range(2):
                for p in range(2):
                    row = y_lo * rows + p * (rows // 2)
                    block = total[row : row + rows // 2, y_hi * 256 : (y_hi + 1) * 256]
                    g[2 * wave + p][x, y_hi, y_lo] = block


def proj_terms(ps, a01, a2, dy, mp, g):
    for x in range(4):
        for t in range(4):
            tile = x * 4 + t
            low = plow(tile)
            spread = dot(dy[:, low : low + PWIN], ps[tile]).astype(BF16)
            for j in range(3):
                mp[j, :, t * 128 : (t + 1) * 128] = spread[:, j * 128 : (j + 1) * 128]
        most = dot(a01[...], mp[0])
        for p in range(2):
            last = dot(a2[...], mp[1 + p])
            for y_lo in range(2):
                row = y_lo * 96 + p * 48
                total = (most[row : row + 48] + last[y_lo * 48 : y_lo * 48 + 48]).astype(BF16)
                for y_hi in range(2):
                    g[4 + p][x, y_hi, y_lo] = total[:, y_hi * 256 : (y_hi + 1) * 256]


class Ring:
    def __init__(self, copy, block, relay, near, place, along):
        self.copy, self.block, self.relay, self.near = copy, block, relay, near
        self.up, self.down = lax.rem(place + 1, 4), lax.rem(place + 3, 4)
        self.two = lax.rem(place + 2, 4)
        self.to_up, self.to_down = along(1), along(3)

    def first(self):
        copy, block, near = self.copy, self.block, self.near
        self.on_way = (
            copy(block(self.two, 0), self.relay.at[0], self.to_up),
            copy(block(self.two, 1), self.relay.at[1], self.to_down),
        )
        self.copies = [
            copy(block(self.up, 1), near.at[0, 1], self.to_up),
            copy(block(self.down, 0), near.at[1, 0], self.to_down),
        ]

    def second(self):
        copy, block, near = self.copy, self.block, self.near
        steps = ((self.up, 0, self.to_up), (self.down, 1, self.to_down))
        for side, (place, half, to) in enumerate(steps):
            self.on_way[side].wait()
            ref = block(place, half)
            ref[...] = (ref[...].astype(F32) + self.relay[side].astype(F32)).astype(BF16)
            self.copies.append(copy(ref, near.at[side, half], to))

    def total(self, own):
        for c in self.copies:
            c.wait()
        near = self.near[0].astype(F32) + self.near[1].astype(F32)
        return own.astype(F32) + near.reshape(own.shape)


class Part:
    def __init__(self, copy, refs, rows, x_first, position, along_x, along_y):
        self.copy, self.rows, self.x_first = copy, rows, x_first
        self.g, relay, near, self.h, self.r = refs
        self.x, self.y_hi, self.y_lo = position
        y = self.y_hi * 2 + self.y_lo
        if x_first:
            self.ring = Ring(copy, self.of_x, relay, near, self.x, along_x)
            self.other, self.along = y, along_y
        else:
            self.ring = Ring(copy, self.of_y, relay, near, y, along_y)
            self.other, self.along = self.x, along_x

    def of_x(self, i, half):
        return self.g.at[i, half]

    def of_y(self, i, half):
        return self.g.at[pl.ds(2 * half, 2), lax.div(i, 2), lax.rem(i, 2)]

    def first(self):
        self.ring.first()

    def second(self):
        self.ring.second()

    def across(self):
        own = self.g[self.x] if self.x_first else self.g[:, self.y_hi, self.y_lo]
        self.h[...] = self.ring.total(own.reshape(4, self.rows, 256)).astype(BF16)
        self.copies = [
            self.copy(self.h.at[lax.rem(self.other + k, 4)], self.r.at[k], self.along(k))
            for k in range(1, 4)
        ]

    def total(self):
        acc = self.h[self.other].astype(F32)
        for k, c in enumerate(self.copies):
            c.wait()
            acc = acc + self.r[k + 1].astype(F32)
        return acc


def kernel(
    x_in, dy_in, ws_in, ps_in, wt_in, pt_in,
    dx_out, sums_out,
    x_v, dy_v, ws, ps, wt, pt,
    nxb, nxr, dxb, dxr, dab, dar, otb, otr,
    qs, ks, vs, os, qt, kt, vt, ot, da, acc0, acc1, acc2, kept_s, kept_t,
    ht, at, hcat, a01, a2, dpk, dyf,
    spread_q, spread_p, mq, mp,
    zs1, zr1, zs2, zr2,
    send, recv, all_send, all_recv, local,
    *part_refs,
):
    dp, me = lax.axis_index("dp"), lax.axis_index("seq")
    core, y_lo = lax.rem(dp, 2), lax.div(dp, 2)
    y_hi, z, x = lax.rem(me, 2), lax.rem(lax.div(me, 2), 8), lax.div(me, 16)
    y = y_hi * 2 + y_lo
    n = GROUPS
    pair = at_xyz(x, y, z, 1 - core)

    def along_x(k):
        return at_xyz(lax.rem(x + k, 4), y, z, core)

    def along_y(k):
        return at_xyz(x, lax.rem(y + k, 4), z, core)

    def along_z(k):
        return at_xyz(x, y, lax.rem(z + k, 8), core)

    counts = [0, 0]

    def here(source, target):
        c = pltpu.make_async_copy(source, target, local.at[counts[0]])
        counts[0] += 1
        c.start()
        return c

    def copy(source, target, to):
        i = counts[1]
        counts[1] += 1
        c = pltpu.make_async_remote_copy(
            src_ref=source,
            dst_ref=target,
            send_sem=send.at[i],
            recv_sem=recv.at[i],
            device_id=to,
            device_id_type=MESH,
        )
        c.start()
        return c

    get_x = here(x_in, x_v)
    get_ws = here(ws_in, ws)
    get_ps = here(ps_in, ps)
    get_dy = here(dy_in, dy_v)
    get_pt = here(pt_in, pt)
    get_wt = here(wt_in, wt)

    barrier = pltpu.get_barrier_semaphore()

    @pl.loop(1, n)
    def _(i):
        pl.semaphore_signal(barrier, inc=1, device_id=(dp, lax.rem(me + i, n)), device_id_type=MESH)

    for friend in (pair, along_y(1), along_y(3)):
        pl.semaphore_signal(barrier, inc=1, device_id=friend, device_id_type=MESH)

    def exchange_start(j, source, target):
        @pl.loop(1, n)
        def _(i):
            to = lax.rem(me + i, n)
            pltpu.make_async_remote_copy(
                src_ref=source.at[to],
                dst_ref=target.at[me],
                send_sem=all_send.at[j],
                recv_sem=all_recv.at[j],
                device_id=(dp, to),
                device_id_type=MESH,
            ).start()

        return here(source.at[me], target.at[me])

    def exchange_wait(j, source, target, own):
        own.wait()
        pltpu.make_async_remote_copy(
            src_ref=source.at[pl.ds(0, n - 1)],
            dst_ref=target.at[pl.ds(0, n - 1)],
            send_sem=all_send.at[j],
            recv_sem=all_recv.at[j],
            device_id=pair,
            device_id_type=MESH,
        ).wait()

    far = pl.ds(TOK, TOK)

    def share_hidden(b):
        copies = []
        for i in range(2):
            for first, rows in WAVES:
                to = pl.ds(2 * first + i * rows, rows)
                row = pl.multiple_of((i * 2 + 1 - core) * QROWS + first, 32)
                copies.append(copy(ht.at[b, pl.ds(row, rows)], hcat.at[b, to, far], pair))
                row = pl.multiple_of((i * 2 + core) * QROWS + first, 32)
                hcat[b, to, :TOK] = ht[b, pl.ds(row, rows), :]
        return copies

    def share_attn(b):
        copies = []
        for i in range(2):
            row = (i * 2 + 1 - core) * 144
            rows = pl.ds(pl.multiple_of(row, 16), 96)
            copies.append(copy(at.at[b, rows], a01.at[b, pl.ds(i * 96, 96), far], pair))
            rows = pl.ds(pl.multiple_of(row + 96, 16), 48)
            copies.append(copy(at.at[b, rows], a2.at[b, pl.ds(i * 48, 48), far], pair))
            row = (i * 2 + core) * 144
            rows = pl.ds(pl.multiple_of(row, 16), 96)
            a01[b, i * 96 : (i + 1) * 96, :TOK] = at[b, rows, :]
            rows = pl.ds(pl.multiple_of(row + 96, 16), 48)
            a2[b, i * 48 : (i + 1) * 48, :TOK] = at[b, rows, :]
        return copies

    def share(ref, b):
        return copy(ref.at[b, pl.ds(0, TOK)], ref.at[b, far], pair)

    def parts(b):
        found = []
        for p, (rows, x_first) in enumerate(PARTS):
            refs = [ref.at[b] for ref in part_refs[p * 5 : (p + 1) * 5]]
            found.append(Part(copy, refs, rows, x_first, (x, y_hi, y_lo), along_x, along_y))
        return found

    def wait(copies):
        for c in copies:
            c.wait()

    def last(b, found, zs, zr):
        total = jnp.concatenate([p.total() for p in found], axis=0).T
        zs[b] = total.reshape(zs.shape[1:]).astype(BF16)
        return [copy(zs.at[b, lax.rem(z + k, 8)], zr.at[b, k], along_z(k)) for k in range(1, 8)]

    def last_first(b, found):
        return last(b, found[:2], zs1, zr1)

    def last_second(b, found):
        return last(b, found[2:], zs2, zr2)

    def finish(b, copies, zs, zr, lanes):
        acc = zs[b, z].astype(F32)
        for k in range(1, 8):
            copies[k - 1].wait()
            acc = acc + zr[b, k].astype(F32)
        sums_out[b, :, lanes] = acc

    def finish_both(b, first, second):
        finish(b, first, zs1, zr1, slice(0, 128))
        finish(b, second, zs2, zr2, slice(128, 384))

    SPACE, TIME = 0, 1
    space, time = parts(SPACE), parts(TIME)
    own = pl.ds(0, TOK)
    accs = (acc0, acc1, acc2)

    get_x.wait()
    source = x_v[...].astype(F32)
    normed, _ = normalize(source)
    hidden = normed.astype(BF16)
    get_ws.wait()
    project(hidden, ws, (qs, ks, vs))
    attention(qs, ks, vs, acc0, os, kept_s, None)
    get_ps.wait()
    to_blocks((source + dot(os[:, :HD], ps[...])).astype(BF16), nxb)
    pl.semaphore_wait(barrier, n + 2)
    own_next = exchange_start(0, nxb, nxr)
    get_dy.wait()
    get_pt.wait()
    da[:, :HD] = dot(dy_v[...], pt[...], NT).astype(BF16)
    da[:, HD:] = jnp.zeros((TOK, PAD - HD), BF16)
    to_blocks(da[...], dab)
    own_da = exchange_start(1, dab, dar)
    dyf[TIME, :TOK, :] = dy_v[...]
    ht[SPACE] = hidden.T
    at[SPACE] = os[...].T
    hidden_s = share_hidden(SPACE)
    proj_s = share_attn(SPACE)
    proj_t = [share(dyf, TIME)]
    spreaders(spread_q, spread_p)

    get_wt.wait()
    exchange_wait(0, nxb, nxr, own_next)
    normed, _ = normalize(from_blocks(nxr).astype(F32))
    hidden = normed.astype(BF16)
    project(hidden, wt, (qt, kt, vt))
    keep = same_position()
    attention(qt, kt, vt, acc0, ot, kept_t, keep)
    to_blocks(ot[...], otb)
    own_attn = exchange_start(3, otb, otr)
    ht[TIME] = hidden.T
    hidden_t = share_hidden(TIME)
    exchange_wait(1, dab, dar, own_da)
    da[...] = from_blocks(dar)
    attention_back(qt, kt, vt, ot, da, accs, kept_t, {})
    pack(accs, dpk.at[TIME, own])
    hidden_t.append(share(dpk, TIME))
    middle = from_blocks(nxr).astype(F32)
    to_blocks(block_back(middle, wt, dpk.at[TIME, own]).astype(BF16), dxb)
    own_dx = exchange_start(2, dxb, dxr)

    def both(found, p, step):
        getattr(found[2 * p], step)()
        getattr(found[2 * p + 1], step)()

    wait(hidden_t)
    qkv_spread(spread_q, dpk.at[TIME], mq, slice(0, 2 * TOK))
    for wave in range(2):
        qkv_terms(wave, hcat.at[TIME], mq, [p.g for p in time])
        both(time, wave, "first")
    exchange_wait(3, otb, otr, own_attn)
    at[TIME] = from_blocks(otr).T
    proj_t += share_attn(TIME)
    wait(proj_t)
    proj_terms(spread_p, a01.at[TIME], a2.at[TIME], dyf.at[TIME], mp, [p.g for p in time])
    both(time, 2, "first")

    exchange_wait(2, dxb, dxr, own_dx)
    dy = (dy_v[...].astype(F32) + from_blocks(dxr).astype(F32)).astype(BF16)
    dyf[SPACE, :TOK, :] = dy
    proj_s.append(share(dyf, SPACE))
    da[:, :HD] = dot(dy, ps[...], NT).astype(BF16)
    da[:, HD:] = jnp.zeros((TOK, PAD - HD), BF16)

    def seconds_qkv():
        both(time, 0, "second")
        both(time, 1, "second")

    def seconds_proj():
        both(time, 2, "second")

    hooks = {0: seconds_qkv, 5: seconds_proj}
    attention_back(qs, ks, vs, os, da, accs, kept_s, hooks)
    pack(accs, dpk.at[SPACE, own])
    hidden_s.append(share(dpk, SPACE))
    qkv_spread(spread_q, dpk.at[SPACE], mq, slice(0, TOK))
    for p in time:
        p.across()
    wait(hidden_s)
    qkv_spread(spread_q, dpk.at[SPACE], mq, slice(TOK, 2 * TOK))
    for wave in range(2):
        qkv_terms(wave, hcat.at[SPACE], mq, [p.g for p in space])
        both(space, wave, "first")
    wait(proj_s)
    proj_terms(spread_p, a01.at[SPACE], a2.at[SPACE], dyf.at[SPACE], mp, [p.g for p in space])
    both(space, 2, "first")
    both(space, 0, "second")
    along_t = last_first(TIME, time), last_second(TIME, time)
    both(space, 1, "second")
    dx_s = block_back(x_v[...].astype(F32), ws, dpk.at[SPACE, own])
    dx_out[...] = (dyf[SPACE, :TOK, :].astype(F32) + dx_s).astype(BF16)
    both(space, 0, "across")
    both(space, 2, "second")
    both(space, 1, "across")
    along_1 = last_first(SPACE, space)
    both(space, 2, "across")
    finish_both(TIME, *along_t)
    finish_both(SPACE, along_1, last_second(SPACE, space))


def outputs_kernel(dx, sums, dx_out, gqs, gps, gqt, gpt):
    dx_out[...] = dx[...]
    for b, (qkv, proj) in enumerate(((gqs, gps), (gqt, gpt))):
        block = sums[b]
        qkv[...] = block[:27, :QROWS]
        proj[:, 0:96] = block[:18, QROWS:]
        proj[0:9, 96:144] = block[18:27, QROWS : QROWS + 48]
        proj[9:18, 96:144] = block[18:27, QROWS + 48 :]


def per_device(latents, out_grad, qkv_spatial, proj_spatial, qkv_temporal, proj_temporal):
    ins = [latents[0, 0], out_grad[0, 0], qkv_spatial, proj_spatial.T, qkv_temporal, proj_temporal.T]
    wide, narrow = VMEM((TOK, D), BF16), VMEM((TOK, PAD), BF16)
    qkv, proj = VMEM((3 * HD, D), BF16), VMEM((HD, D), BF16)
    blocks = VMEM((GROUPS, D // 128, OWN, 128), BF16)
    small = VMEM((GROUPS, PAD // 128, OWN, 128), BF16)
    acc = VMEM((TOK, PAD), F32)
    dma = pltpu.SemaphoreType.DMA
    part_refs = []
    for rows, _ in PARTS:
        part_refs += [
            VMEM((2, 4, 2, 2, rows, 256), BF16),
            VMEM((2, 2, 2, rows, 256), BF16),
            VMEM((2, 2, 2, 2, rows, 256), BF16),
            VMEM((2, 4, rows, 256), BF16),
            VMEM((2, 4, rows, 256), BF16),
        ]
    dx, sums = pl.pallas_call(
        kernel,
        out_shape=[
            jax.ShapeDtypeStruct((TOK, D), BF16),
            jax.ShapeDtypeStruct((2, 32, ROWS), F32),
        ],
        in_specs=[pl.BlockSpec(memory_space=pl.ANY)] * len(ins),
        out_specs=[pl.BlockSpec(memory_space=VMEM)] * 2,
        scratch_shapes=[
            wide, wide, qkv, proj, qkv, proj,
            *[blocks] * 4, *[small] * 4,
            *[narrow] * 9, acc, acc, acc,
            *[VMEM((HEADS, TOK, TOK), BF16)] * 2,
            VMEM((2, D, TOK), BF16),
            VMEM((2, PAD, TOK), BF16),
            VMEM((2, 2 * QROWS, 2 * TOK), BF16),
            VMEM((2, 192, 2 * TOK), BF16),
            VMEM((2, 96, 2 * TOK), BF16),
            VMEM((2, 2 * TOK, WIDE), BF16),
            VMEM((2, 2 * TOK, D), BF16),
            VMEM((TILES, QWIN, 128), BF16),
            VMEM((TILES, PWIN, 384), BF16),
            VMEM((2 * TOK, TILES * 128), BF16),
            VMEM((3, 2 * TOK, 512), BF16),
            *[VMEM((2, 8, 32, 128), BF16)] * 2,
            *[VMEM((2, 8, 32, 256), BF16)] * 2,
            dma((156,)), dma((156,)), dma((4,)), dma((4,)), dma((10,)),
            *part_refs,
        ],
        name="both_blocks",
        compiler_params=pltpu.CompilerParams(
            collective_id=0, has_side_effects=True, vmem_limit_bytes=LIMIT
        ),
    )(*ins)
    vmem = pl.BlockSpec(memory_space=VMEM)
    f32 = [jax.ShapeDtypeStruct(s, F32) for s in ((27, 288), (18, 144), (27, 288), (18, 144))]
    dx, qkv_s, proj_s, qkv_t, proj_t = pl.pallas_call(
        outputs_kernel,
        out_shape=[jax.ShapeDtypeStruct((TOK, D), BF16), *f32],
        in_specs=[vmem] * 2,
        out_specs=[vmem] * 5,
        name="outputs",
    )(dx, sums)
    return dx[None, None], qkv_s, proj_s, qkv_t, proj_t


def solution(mesh):
    placed = (P("dp", "seq", None, None), P("dp", "seq", None, None), P(), P(), P(), P())
    return jax.shard_map(
        per_device,
        mesh=mesh,
        in_specs=placed,
        out_specs=(
            P("dp", "seq", None, None),
            P("seq", "dp"),
            P("seq", "dp"),
            P("seq", "dp"),
            P("seq", "dp"),
        ),
        check_vma=False,
    )
```

```python
import jax
import jax.numpy as jnp
from jax import lax
from jax.experimental import pallas as pl
from jax.experimental.pallas import tpu as pltpu
from jax.sharding import PartitionSpec as P

HDIM = 72
HEADS = 8
HD = HDIM * HEADS
PAD = 640
D = 1152
TOK = 256
GROUPS = 64
OWN = TOK // GROUPS
EPS = 1e-06
SCALE = HDIM ** (-0.5)
NEG = -1e30
MESH = pl.DeviceIdType.MESH
VMEM = pltpu.VMEM
F32 = jnp.float32
BF16 = jnp.bfloat16
LIMIT = 60 * 2**20

QROWS = 288
PROWS = 96
ROWS = QROWS + PROWS
PARTS = ((64, True), (64, False), (80, True), (80, False), (48, True), (48, False))
WAVES = ((0, 128), (128, 160))
TILES = 16
QWIN = 384
PWIN = 256
WIDE = 1792


def dot(a, b, dims=((1,), (0,))):
    return lax.dot_general(a, b, (dims, ((), ())), preferred_element_type=F32)


NT = ((1,), (1,))
TN = ((0,), (0,))


def window(head):
    low = head * HDIM // 128 * 128
    return low, -(-(head + 1) * HDIM // 128) * 128


def head_mask(head, low, high):
    lane = lax.broadcasted_iota(jnp.int32, (1, high - low), 1) + low
    return ((lane >= head * HDIM) & (lane < (head + 1) * HDIM)).astype(F32).astype(BF16)


def normalize(x):
    inverse = lax.rsqrt(jnp.mean(x * x, axis=-1, keepdims=True) + EPS)
    return x * inverse, inverse


def project(hidden, w_ref, targets):
    for i, target in enumerate(targets):
        target[:, :HD] = dot(hidden, w_ref[i * HD : (i + 1) * HD, :], NT).astype(BF16)
        target[:, HD:] = jnp.zeros((TOK, PAD - HD), BF16)


def softmax(qm, k, keep):
    s = dot(qm, k, NT) * SCALE
    if keep is not None:
        s = jnp.where(keep, s, NEG)
    e = jnp.exp(s - jnp.max(s, axis=-1, keepdims=True))
    return e * (1.0 / jnp.sum(e, axis=-1, keepdims=True))


def same_position():
    rows = lax.broadcasted_iota(jnp.int32, (TOK, TOK), 0)
    columns = lax.broadcasted_iota(jnp.int32, (TOK, TOK), 1)
    return lax.rem(rows, OWN) == lax.rem(columns, OWN)


def attention(q, k, v, acc, attn, kept, keep):
    acc[...] = jnp.zeros_like(acc)
    for h in range(HEADS):
        low, high = window(h)
        mask = head_mask(h, low, high)
        probs = softmax(q[:, low:high] * mask, k[:, low:high], keep)
        kept[h] = probs.astype(BF16)
        acc[:, low:high] += dot(kept[h], v[:, low:high] * mask)
    attn[...] = acc[...].astype(BF16)


def attention_back(q, k, v, attn, da, accs, kept, hooks):
    for acc in accs:
        acc[...] = jnp.zeros_like(acc)
    dq, dk, dv = accs
    for h in range(HEADS):
        if h in hooks:
            hooks[h]()
        low, high = window(h)
        mask = head_mask(h, low, high)
        qm = q[:, low:high] * mask
        km = k[:, low:high] * mask
        dam = da[:, low:high] * mask
        d_probs = dot(dam, v[:, low:high], NT)
        dv[:, low:high] += dot(kept[h], dam, TN)
        offset = jnp.sum(dam.astype(F32) * attn[:, low:high].astype(F32), axis=-1, keepdims=True)
        ds = (kept[h].astype(F32) * ((d_probs - offset) * SCALE)).astype(BF16)
        dq[:, low:high] += dot(ds, km)
        dk[:, low:high] += dot(ds, qm, TN)


def pack(accs, dpk):
    for i, acc in enumerate(accs):
        dpk[:, i * HD : (i + 1) * HD] = acc[:, :HD].astype(BF16)
    dpk[:, 3 * HD :] = jnp.zeros((TOK, WIDE - 3 * HD), BF16)


def block_back(x, w_ref, dpk):
    d_hidden = dot(dpk[:, : 3 * HD], w_ref[...])
    normed, inverse = normalize(x)
    along = jnp.mean(d_hidden * normed, axis=-1, keepdims=True)
    return inverse * (d_hidden - normed * along)


def to_blocks(value, ref):
    for t in range(ref.shape[1]):
        ref[:, t, :, :] = value[:, t * 128 : (t + 1) * 128].reshape(GROUPS, OWN, 128)


def from_blocks(ref):
    return jnp.concatenate([ref[:, t, :, :].reshape(TOK, 128) for t in range(ref.shape[1])], axis=1)


def at_xyz(x, y, z, core):
    return lax.rem(y, 2) * 2 + core, (x * 8 + z) * 2 + lax.div(y, 2)


def lane_shards(tile):
    x, y_hi, z_hi = tile // 4, tile // 2 % 2, tile % 2
    return [(x * 8 + z_hi * 4 + i) * 2 + y_hi for i in range(4)]


def qlow(tile):
    return min(27 * lane_shards(tile)[0] // 128 * 128, WIDE - QWIN)


def plow(tile):
    return min(18 * lane_shards(tile)[0] // 128 * 128, D - PWIN)


def choice(low, window, lead, first, count, step):
    row = lax.broadcasted_iota(jnp.int32, (window, 128), 0) + low
    lane = lax.broadcasted_iota(jnp.int32, (1, 128), 1)
    inner = (lane & 31) - first
    wanted = lead + lax.shift_right_logical(lane, 5) * step + inner
    wanted = jnp.where((inner >= 0) & (inner < count), wanted, -1)
    return (row == wanted).astype(F32).astype(BF16)


def spreaders(qs, ps):
    for tile in range(TILES):
        shard = lane_shards(tile)[0]
        qs[tile] = choice(qlow(tile), QWIN, 27 * shard, 0, 27, 54)
        low = plow(tile)
        ps[tile, :, 0:128] = choice(low, PWIN, 18 * shard, 0, 18, 36)
        ps[tile, :, 128:256] = choice(low, PWIN, 18 * shard, 18, 9, 36)
        ps[tile, :, 256:384] = choice(low, PWIN, 18 * shard + 9, 18, 9, 36)


def qkv_spread(qs, dpk, mq, rows):
    for tile in range(TILES):
        low = qlow(tile)
        spread = dot(dpk[rows, low : low + QWIN], qs[tile])
        mq[rows, tile * 128 : (tile + 1) * 128] = spread.astype(BF16)


def qkv_terms(wave, hcat, mq, g):
    first, rows = WAVES[wave]
    for x in range(4):
        total = dot(hcat[2 * first : 2 * (first + rows)], mq[:, x * 512 : (x + 1) * 512])
        total = total.astype(BF16)
        for y_lo in range(2):
            for y_hi in range(2):
                for p in range(2):
                    row = y_lo * rows + p * (rows // 2)
                    block = total[row : row + rows // 2, y_hi * 256 : (y_hi + 1) * 256]
                    g[2 * wave + p][x, y_hi, y_lo] = block


def proj_terms(ps, a01, a2, dy, mp, g):
    for x in range(4):
        for t in range(4):
            tile = x * 4 + t
            low = plow(tile)
            spread = dot(dy[:, low : low + PWIN], ps[tile]).astype(BF16)
            for j in range(3):
                mp[j, :, t * 128 : (t + 1) * 128] = spread[:, j * 128 : (j + 1) * 128]
        most = dot(a01[...], mp[0])
        for p in range(2):
            last = dot(a2[...], mp[1 + p])
            for y_lo in range(2):
                row = y_lo * 96 + p * 48
                total = (most[row : row + 48] + last[y_lo * 48 : y_lo * 48 + 48]).astype(BF16)
                for y_hi in range(2):
                    g[4 + p][x, y_hi, y_lo] = total[:, y_hi * 256 : (y_hi + 1) * 256]


class Ring:
    def __init__(self, copy, block, relay, near, place, along):
        self.copy, self.block, self.relay, self.near = copy, block, relay, near
        self.up, self.down = lax.rem(place + 1, 4), lax.rem(place + 3, 4)
        self.two = lax.rem(place + 2, 4)
        self.to_up, self.to_down = along(1), along(3)

    def first(self):
        copy, block, near = self.copy, self.block, self.near
        self.on_way = (
            copy(block(self.two, 0), self.relay.at[0], self.to_up),
            copy(block(self.two, 1), self.relay.at[1], self.to_down),
        )
        self.copies = [
            copy(block(self.up, 1), near.at[0, 1], self.to_up),
            copy(block(self.down, 0), near.at[1, 0], self.to_down),
        ]

    def second(self):
        copy, block, near = self.copy, self.block, self.near
        steps = ((self.up, 0, self.to_up), (self.down, 1, self.to_down))
        for side, (place, half, to) in enumerate(steps):
            self.on_way[side].wait()
            ref = block(place, half)
            ref[...] = (ref[...].astype(F32) + self.relay[side].astype(F32)).astype(BF16)
            self.copies.append(copy(ref, near.at[side, half], to))

    def total(self, own):
        for c in self.copies:
            c.wait()
        near = self.near[0].astype(F32) + self.near[1].astype(F32)
        return own.astype(F32) + near.reshape(own.shape)


class Part:
    def __init__(self, copy, refs, rows, x_first, position, along_x, along_y):
        self.copy, self.rows, self.x_first = copy, rows, x_first
        self.g, relay, near, self.h, self.r = refs
        self.x, self.y_hi, self.y_lo = position
        y = self.y_hi * 2 + self.y_lo
        if x_first:
            self.ring = Ring(copy, self.of_x, relay, near, self.x, along_x)
            self.other, self.along = y, along_y
        else:
            self.ring = Ring(copy, self.of_y, relay, near, y, along_y)
            self.other, self.along = self.x, along_x

    def of_x(self, i, half):
        return self.g.at[i, half]

    def of_y(self, i, half):
        return self.g.at[pl.ds(2 * half, 2), lax.div(i, 2), lax.rem(i, 2)]

    def first(self):
        self.ring.first()

    def second(self):
        self.ring.second()

    def across(self):
        own = self.g[self.x] if self.x_first else self.g[:, self.y_hi, self.y_lo]
        self.h[...] = self.ring.total(own.reshape(4, self.rows, 256)).astype(BF16)
        self.copies = [
            self.copy(self.h.at[lax.rem(self.other + k, 4)], self.r.at[k], self.along(k))
            for k in range(1, 4)
        ]

    def total(self):
        acc = self.h[self.other].astype(F32)
        for k, c in enumerate(self.copies):
            c.wait()
            acc = acc + self.r[k + 1].astype(F32)
        return acc


def kernel(
    x_in, dy_in, ws_in, ps_in, wt_in, pt_in,
    dx_out, sums_out,
    x_v, dy_v, ws, ps, wt, pt,
    nxb, nxr, dxb, dxr, dab, dar, otb, otr,
    qs, ks, vs, os, qt, kt, vt, ot, da, acc0, acc1, acc2, kept_s, kept_t,
    ht, at, hcat, a01, a2, dpk, dyf,
    spread_q, spread_p, mq, mp,
    zs1, zr1, zs2, zr2,
    send, recv, all_send, all_recv, local,
    *part_refs,
):
    dp, me = lax.axis_index("dp"), lax.axis_index("seq")
    core, y_lo = lax.rem(dp, 2), lax.div(dp, 2)
    y_hi, z, x = lax.rem(me, 2), lax.rem(lax.div(me, 2), 8), lax.div(me, 16)
    y = y_hi * 2 + y_lo
    n = GROUPS
    pair = at_xyz(x, y, z, 1 - core)

    def along_x(k):
        return at_xyz(lax.rem(x + k, 4), y, z, core)

    def along_y(k):
        return at_xyz(x, lax.rem(y + k, 4), z, core)

    def along_z(k):
        return at_xyz(x, y, lax.rem(z + k, 8), core)

    counts = [0, 0]

    def here(source, target):
        c = pltpu.make_async_copy(source, target, local.at[counts[0]])
        counts[0] += 1
        c.start()
        return c

    def copy(source, target, to):
        i = counts[1]
        counts[1] += 1
        c = pltpu.make_async_remote_copy(
            src_ref=source,
            dst_ref=target,
            send_sem=send.at[i],
            recv_sem=recv.at[i],
            device_id=to,
            device_id_type=MESH,
        )
        c.start()
        return c

    get_x = here(x_in, x_v)
    get_ws = here(ws_in, ws)
    get_ps = here(ps_in, ps)
    get_dy = here(dy_in, dy_v)
    get_pt = here(pt_in, pt)
    get_wt = here(wt_in, wt)

    barrier = pltpu.get_barrier_semaphore()

    @pl.loop(1, n)
    def _(i):
        pl.semaphore_signal(barrier, inc=1, device_id=(dp, lax.rem(me + i, n)), device_id_type=MESH)

    for friend in (pair, along_y(1), along_y(3)):
        pl.semaphore_signal(barrier, inc=1, device_id=friend, device_id_type=MESH)

    def exchange_start(j, source, target):
        @pl.loop(1, n)
        def _(i):
            to = lax.rem(me + i, n)
            pltpu.make_async_remote_copy(
                src_ref=source.at[to],
                dst_ref=target.at[me],
                send_sem=all_send.at[j],
                recv_sem=all_recv.at[j],
                device_id=(dp, to),
                device_id_type=MESH,
            ).start()

        return here(source.at[me], target.at[me])

    def exchange_wait(j, source, target, own):
        own.wait()
        pltpu.make_async_remote_copy(
            src_ref=source.at[pl.ds(0, n - 1)],
            dst_ref=target.at[pl.ds(0, n - 1)],
            send_sem=all_send.at[j],
            recv_sem=all_recv.at[j],
            device_id=pair,
            device_id_type=MESH,
        ).wait()

    far = pl.ds(TOK, TOK)

    def share_hidden(b):
        copies = []
        for i in range(2):
            for first, rows in WAVES:
                to = pl.ds(2 * first + i * rows, rows)
                row = pl.multiple_of((i * 2 + 1 - core) * QROWS + first, 32)
                copies.append(copy(ht.at[b, pl.ds(row, rows)], hcat.at[b, to, far], pair))
                row = pl.multiple_of((i * 2 + core) * QROWS + first, 32)
                hcat[b, to, :TOK] = ht[b, pl.ds(row, rows), :]
        return copies

    def share_attn(b):
        copies = []
        for i in range(2):
            row = (i * 2 + 1 - core) * 144
            rows = pl.ds(pl.multiple_of(row, 16), 96)
            copies.append(copy(at.at[b, rows], a01.at[b, pl.ds(i * 96, 96), far], pair))
            rows = pl.ds(pl.multiple_of(row + 96, 16), 48)
            copies.append(copy(at.at[b, rows], a2.at[b, pl.ds(i * 48, 48), far], pair))
            row = (i * 2 + core) * 144
            rows = pl.ds(pl.multiple_of(row, 16), 96)
            a01[b, i * 96 : (i + 1) * 96, :TOK] = at[b, rows, :]
            rows = pl.ds(pl.multiple_of(row + 96, 16), 48)
            a2[b, i * 48 : (i + 1) * 48, :TOK] = at[b, rows, :]
        return copies

    def share(ref, b):
        return copy(ref.at[b, pl.ds(0, TOK)], ref.at[b, far], pair)

    def parts(b):
        found = []
        for p, (rows, x_first) in enumerate(PARTS):
            refs = [ref.at[b] for ref in part_refs[p * 5 : (p + 1) * 5]]
            found.append(Part(copy, refs, rows, x_first, (x, y_hi, y_lo), along_x, along_y))
        return found

    def wait(copies):
        for c in copies:
            c.wait()

    def last(b, found, zs, zr):
        total = jnp.concatenate([p.total() for p in found], axis=0).T
        zs[b] = total.reshape(zs.shape[1:]).astype(BF16)
        return [copy(zs.at[b, lax.rem(z + k, 8)], zr.at[b, k], along_z(k)) for k in range(1, 8)]

    def last_first(b, found):
        return last(b, found[:2], zs1, zr1)

    def last_second(b, found):
        return last(b, found[2:], zs2, zr2)

    def finish(b, copies, zs, zr, lanes):
        acc = zs[b, z].astype(F32)
        for k in range(1, 8):
            copies[k - 1].wait()
            acc = acc + zr[b, k].astype(F32)
        sums_out[b, :, lanes] = acc

    def finish_both(b, first, second):
        finish(b, first, zs1, zr1, slice(0, 128))
        finish(b, second, zs2, zr2, slice(128, 384))

    SPACE, TIME = 0, 1
    space, time = parts(SPACE), parts(TIME)
    own = pl.ds(0, TOK)
    accs = (acc0, acc1, acc2)

    get_x.wait()
    source = x_v[...].astype(F32)
    normed, _ = normalize(source)
    hidden = normed.astype(BF16)
    get_ws.wait()
    project(hidden, ws, (qs, ks, vs))
    attention(qs, ks, vs, acc0, os, kept_s, None)
    get_ps.wait()
    to_blocks((source + dot(os[:, :HD], ps[...])).astype(BF16), nxb)
    pl.semaphore_wait(barrier, n + 2)
    own_next = exchange_start(0, nxb, nxr)
    get_dy.wait()
    get_pt.wait()
    da[:, :HD] = dot(dy_v[...], pt[...], NT).astype(BF16)
    da[:, HD:] = jnp.zeros((TOK, PAD - HD), BF16)
    to_blocks(da[...], dab)
    own_da = exchange_start(1, dab, dar)
    dyf[TIME, :TOK, :] = dy_v[...]
    ht[SPACE] = hidden.T
    at[SPACE] = os[...].T
    hidden_s = share_hidden(SPACE)
    proj_s = share_attn(SPACE)
    proj_t = [share(dyf, TIME)]
    spreaders(spread_q, spread_p)

    get_wt.wait()
    exchange_wait(0, nxb, nxr, own_next)
    normed, _ = normalize(from_blocks(nxr).astype(F32))
    hidden = normed.astype(BF16)
    project(hidden, wt, (qt, kt, vt))
    keep = same_position()
    attention(qt, kt, vt, acc0, ot, kept_t, keep)
    to_blocks(ot[...], otb)
    own_attn = exchange_start(3, otb, otr)
    ht[TIME] = hidden.T
    hidden_t = share_hidden(TIME)
    exchange_wait(1, dab, dar, own_da)
    da[...] = from_blocks(dar)
    attention_back(qt, kt, vt, ot, da, accs, kept_t, {})
    pack(accs, dpk.at[TIME, own])
    hidden_t.append(share(dpk, TIME))
    middle = from_blocks(nxr).astype(F32)
    to_blocks(block_back(middle, wt, dpk.at[TIME, own]).astype(BF16), dxb)
    own_dx = exchange_start(2, dxb, dxr)

    def both(found, p, step):
        getattr(found[2 * p], step)()
        getattr(found[2 * p + 1], step)()

    wait(hidden_t)
    qkv_spread(spread_q, dpk.at[TIME], mq, slice(0, 2 * TOK))
    for wave in range(2):
        qkv_terms(wave, hcat.at[TIME], mq, [p.g for p in time])
        both(time, wave, "first")
    exchange_wait(3, otb, otr, own_attn)
    at[TIME] = from_blocks(otr).T
    proj_t += share_attn(TIME)
    wait(proj_t)
    proj_terms(spread_p, a01.at[TIME], a2.at[TIME], dyf.at[TIME], mp, [p.g for p in time])
    both(time, 2, "first")

    exchange_wait(2, dxb, dxr, own_dx)
    dy = (dy_v[...].astype(F32) + from_blocks(dxr).astype(F32)).astype(BF16)
    dyf[SPACE, :TOK, :] = dy
    proj_s.append(share(dyf, SPACE))
    da[:, :HD] = dot(dy, ps[...], NT).astype(BF16)
    da[:, HD:] = jnp.zeros((TOK, PAD - HD), BF16)

    def seconds_qkv():
        both(time, 0, "second")
        both(time, 1, "second")

    def seconds_proj():
        both(time, 2, "second")

    hooks = {0: seconds_qkv, 5: seconds_proj}
    attention_back(qs, ks, vs, os, da, accs, kept_s, hooks)
    pack(accs, dpk.at[SPACE, own])
    hidden_s.append(share(dpk, SPACE))
    qkv_spread(spread_q, dpk.at[SPACE], mq, slice(0, TOK))
    for p in time:
        p.across()
    wait(hidden_s)
    qkv_spread(spread_q, dpk.at[SPACE], mq, slice(TOK, 2 * TOK))
    for wave in range(2):
        qkv_terms(wave, hcat.at[SPACE], mq, [p.g for p in space])
        both(space, wave, "first")
    wait(proj_s)
    proj_terms(spread_p, a01.at[SPACE], a2.at[SPACE], dyf.at[SPACE], mp, [p.g for p in space])
    both(space, 2, "first")
    both(space, 0, "second")
    along_t = last_first(TIME, time), last_second(TIME, time)
    both(space, 1, "second")
    both(space, 0, "across")
    both(space, 2, "second")
    both(space, 1, "across")
    along_1 = last_first(SPACE, space)
    both(space, 2, "across")
    along_2 = last_second(SPACE, space)
    dx_s = block_back(x_v[...].astype(F32), ws, dpk.at[SPACE, own])
    dx_out[...] = (dyf[SPACE, :TOK, :].astype(F32) + dx_s).astype(BF16)
    finish_both(TIME, *along_t)
    finish_both(SPACE, along_1, along_2)


def outputs_kernel(dx, sums, dx_out, gqs, gps, gqt, gpt):
    dx_out[...] = dx[...]
    for b, (qkv, proj) in enumerate(((gqs, gps), (gqt, gpt))):
        block = sums[b]
        qkv[...] = block[:27, :QROWS]
        proj[:, 0:96] = block[:18, QROWS:]
        proj[0:9, 96:144] = block[18:27, QROWS : QROWS + 48]
        proj[9:18, 96:144] = block[18:27, QROWS + 48 :]


def per_device(latents, out_grad, qkv_spatial, proj_spatial, qkv_temporal, proj_temporal):
    ins = [latents[0, 0], out_grad[0, 0], qkv_spatial, proj_spatial.T, qkv_temporal, proj_temporal.T]
    wide, narrow = VMEM((TOK, D), BF16), VMEM((TOK, PAD), BF16)
    qkv, proj = VMEM((3 * HD, D), BF16), VMEM((HD, D), BF16)
    blocks = VMEM((GROUPS, D // 128, OWN, 128), BF16)
    small = VMEM((GROUPS, PAD // 128, OWN, 128), BF16)
    acc = VMEM((TOK, PAD), F32)
    dma = pltpu.SemaphoreType.DMA
    part_refs = []
    for rows, _ in PARTS:
        part_refs += [
            VMEM((2, 4, 2, 2, rows, 256), BF16),
            VMEM((2, 2, 2, rows, 256), BF16),
            VMEM((2, 2, 2, 2, rows, 256), BF16),
            VMEM((2, 4, rows, 256), BF16),
            VMEM((2, 4, rows, 256), BF16),
        ]
    dx, sums = pl.pallas_call(
        kernel,
        out_shape=[
            jax.ShapeDtypeStruct((TOK, D), BF16),
            jax.ShapeDtypeStruct((2, 32, ROWS), F32),
        ],
        in_specs=[pl.BlockSpec(memory_space=pl.ANY)] * len(ins),
        out_specs=[pl.BlockSpec(memory_space=VMEM)] * 2,
        scratch_shapes=[
            wide, wide, qkv, proj, qkv, proj,
            *[blocks] * 4, *[small] * 4,
            *[narrow] * 9, acc, acc, acc,
            *[VMEM((HEADS, TOK, TOK), BF16)] * 2,
            VMEM((2, D, TOK), BF16),
            VMEM((2, PAD, TOK), BF16),
            VMEM((2, 2 * QROWS, 2 * TOK), BF16),
            VMEM((2, 192, 2 * TOK), BF16),
            VMEM((2, 96, 2 * TOK), BF16),
            VMEM((2, 2 * TOK, WIDE), BF16),
            VMEM((2, 2 * TOK, D), BF16),
            VMEM((TILES, QWIN, 128), BF16),
            VMEM((TILES, PWIN, 384), BF16),
            VMEM((2 * TOK, TILES * 128), BF16),
            VMEM((3, 2 * TOK, 512), BF16),
            *[VMEM((2, 8, 32, 128), BF16)] * 2,
            *[VMEM((2, 8, 32, 256), BF16)] * 2,
            dma((156,)), dma((156,)), dma((4,)), dma((4,)), dma((10,)),
            *part_refs,
        ],
        name="both_blocks",
        compiler_params=pltpu.CompilerParams(
            collective_id=0, has_side_effects=True, vmem_limit_bytes=LIMIT
        ),
    )(*ins)
    vmem = pl.BlockSpec(memory_space=VMEM)
    f32 = [jax.ShapeDtypeStruct(s, F32) for s in ((27, 288), (18, 144), (27, 288), (18, 144))]
    dx, qkv_s, proj_s, qkv_t, proj_t = pl.pallas_call(
        outputs_kernel,
        out_shape=[jax.ShapeDtypeStruct((TOK, D), BF16), *f32],
        in_specs=[vmem] * 2,
        out_specs=[vmem] * 5,
        name="outputs",
    )(dx, sums)
    return dx[None, None], qkv_s, proj_s, qkv_t, proj_t


def solution(mesh):
    placed = (P("dp", "seq", None, None), P("dp", "seq", None, None), P(), P(), P(), P())
    return jax.shard_map(
        per_device,
        mesh=mesh,
        in_specs=placed,
        out_specs=(
            P("dp", "seq", None, None),
            P("seq", "dp"),
            P("seq", "dp"),
            P("seq", "dp"),
            P("seq", "dp"),
        ),
        check_vma=False,
    )
```
